512 devices in a mesh: ctx: 64 (over y_hi, z, core), head: 8 (over y_lo, x).
Axes of the slice: x: 4, y: 8 (y_hi: 4, y_lo: 2; y = y_hi * 2 + y_lo), z: 8, core: 2. Of those that a mesh axis runs over, the one named last changes fastest.
Arguments:
- queries: bfloat16 [8192, 6144], P('ctx', 'head'), may hold values from -12 to 12
- keys: bfloat16 [8192, 1024], P('ctx', 'head'), may hold values from -12 to 12
- values: bfloat16 [8192, 1024], P('ctx', 'head'), may hold values from -6 to 6
- output_cotangent: bfloat16 [8192, 6144], P('ctx', 'head'), may hold values from -3 to 3
- lengths: int32 [16], replicated, may hold values from 1 to 4096, 8192 in all
- send_order: int32 [64, 128], P('ctx'), may hold values from 0 to 127, each once within a row
Outputs:
- dq_owned: bfloat16 [8192, 6144], P('ctx', 'head')
- key_gradient_home: bfloat16 [8192, 1024], P('ctx', 'head')
- value_gradient_home: bfloat16 [8192, 1024], P('ctx', 'head')
The draws below stay inside these ranges and needn't reach their ends.
Inputs may be any that keep to these rules, and one draw needn't show every extreme that they name: The lengths sum to 8192; the longest is exactly 4096. `send_order`: each row is a permutation of 0 to 127.
All inputs are finite; a program needn't handle non-finite values.
Results may differ from the reference program's by a relative error of at most 0.005.
Values may be sent and summed in bfloat16 or wider, within the bound.
A program may use at most 64 MiB of HBM per device.

```python
import math
import jax
import jax.numpy as jnp
import numpy as np
from jax import lax

QUERY_HEADS = 48
KEY_VALUE_HEADS = 8
HEAD_SIZE = 128
SOFTCAP = 30
TOK_DEV = 128
DOCS = 16
TOKEN_COUNT = 8192
MOST_DOC = 4096
N_CTX = 64


def level_of(stream_key, dims, cuts, smallest, high):
    def one(axis_at, blocks):
        draws = jax.random.uniform(jax.random.fold_in(jax.random.fold_in(stream_key, 6), axis_at), (blocks,), jnp.float32, smallest / len(cuts), high / len(cuts))
        return jnp.repeat(jnp.exp(draws), dims[axis_at] // blocks).reshape((-1,) + (1,) * (len(dims) - axis_at - 1))

    level = one(*cuts[0])
    for cut in cuts[1:]:
        level = level * one(*cut)
    return level


def length_profile(count, total, most, skew):
    portions = [(1 << 20) // math.isqrt(rank ** skew) + 1 for rank in range(2, count + 1)]
    rest, holding = total - most - (count - 1), [1] * (count - 1)
    while rest > 0:
        movable = [i for i in range(count - 1) if holding[i] < most]
        whole, remaining = sum([portions[i] for i in movable]), rest
        for i in movable:
            more = min(most - holding[i], max(1, remaining * portions[i] // whole), rest)
            holding[i] = holding[i] + more
            rest = rest - more
    return np.array([most] + holding)


def ragged_sizes(rng, number_of, total, most, slope):
    if number_of == 2:
        one = jax.random.randint(rng, (), max(1, total - most), min(most, total - 1) + 1)
        return jnp.stack([one, total - one])
    sizes = jnp.asarray(length_profile(number_of, total, most, slope), jnp.int32)
    pairs = (number_of - 1) // 2
    donor, receiver = sizes[1:1 + 2 * pairs:2], sizes[2:2 + 2 * pairs:2]
    margin = jnp.minimum(donor - 1, most - receiver)
    passed = jax.random.randint(jax.random.fold_in(rng, 1), (pairs,), 0, 1 << 20) % (margin + 1)
    sizes = sizes.at[1:1 + 2 * pairs:2].set(donor - passed).at[2:2 + 2 * pairs:2].set(receiver + passed)
    return sizes[jax.random.permutation(jax.random.fold_in(rng, 2), number_of)]


def normal_values(rng, extent, spread, most, pieces=(), kind=jnp.bfloat16):
    array = spread * jax.random.normal(rng, extent, jnp.float32)
    if pieces:
        array = array * level_of(rng, extent, pieces, -0.22, 0.18)
    return jnp.clip(array, -most, most).astype(kind)


def setup_inputs(seed: int = 0) -> dict:
    streams_of = jax.random.split(jax.random.key(seed), 7)
    queries = normal_values(streams_of[0], (TOKEN_COUNT, QUERY_HEADS * HEAD_SIZE), 2.0, 12.0, ((0, 64), (1, 8)))
    keys = normal_values(streams_of[1], (TOKEN_COUNT, KEY_VALUE_HEADS * HEAD_SIZE), 2.0, 12.0, ((0, 64), (1, 8)))
    values = normal_values(streams_of[2], (TOKEN_COUNT, KEY_VALUE_HEADS * HEAD_SIZE), 1.0, 6.0, ((0, 64), (1, 8)))
    output_cotangent = normal_values(streams_of[3], (TOKEN_COUNT, QUERY_HEADS * HEAD_SIZE), 0.5, 3.0, ((0, 64), (1, 8)))
    lengths = ragged_sizes(streams_of[4], DOCS, TOKEN_COUNT, MOST_DOC, 2).astype(jnp.int32)
    send_order = jax.vmap(lambda own: jax.random.permutation(own, TOK_DEV))(jax.random.split(streams_of[5], N_CTX)).reshape((N_CTX, TOK_DEV)).astype(jnp.int32)
    return {"queries": queries, "keys": keys, "values": values, "output_cotangent": output_cotangent, "lengths": lengths, "send_order": send_order}


KEYS_PER_TILE = 512


def doc_starts(lengths, positions):
    starts = jnp.cumsum(lengths).astype(jnp.int32) - lengths
    before = positions[:, None] >= starts[None, :]
    return jnp.max(jnp.where(before, starts[None, :], 0), axis=1).astype(jnp.int32)


def score_tile(q_block, d_block, key_tile, value_tile, q_pos, q_start, k_pos):
    logit_scale = HEAD_SIZE ** -0.5
    raw_scores = jnp.einsum("rngd,knd->rngk", q_block.astype(jnp.float32), key_tile.astype(jnp.float32)) * logit_scale
    bent = jnp.tanh(raw_scores / SOFTCAP)
    scores = SOFTCAP * bent
    visible = (k_pos[None, :] >= q_start[:, None]) & (k_pos[None, :] <= q_pos[:, None])
    dots = jnp.einsum("rngd,knd->rngk", d_block.astype(jnp.float32), value_tile.astype(jnp.float32))
    return bent, scores, visible[:, None, None, :], dots


def reference(queries, keys, values, output_cotangent, lengths, send_order):
    queries_per_key_head = QUERY_HEADS // KEY_VALUE_HEADS
    logit_scale = HEAD_SIZE ** -0.5
    blocks = TOKEN_COUNT // KEYS_PER_TILE
    positions = jnp.arange(TOKEN_COUNT, dtype=jnp.int32)
    starts_all = doc_starts(lengths, positions)
    query_four = queries.reshape(TOKEN_COUNT, KEY_VALUE_HEADS, queries_per_key_head, HEAD_SIZE)
    output_grad_four = output_cotangent.reshape(TOKEN_COUNT, KEY_VALUE_HEADS, queries_per_key_head, HEAD_SIZE)
    key_three = keys.reshape(TOKEN_COUNT, KEY_VALUE_HEADS, HEAD_SIZE)
    value_three = values.reshape(TOKEN_COUNT, KEY_VALUE_HEADS, HEAD_SIZE)
    empty_row_stat = jnp.zeros((KEYS_PER_TILE, KEY_VALUE_HEADS, queries_per_key_head), jnp.float32)
    empty_query_gradient = jnp.zeros((KEYS_PER_TILE, KEY_VALUE_HEADS, queries_per_key_head, HEAD_SIZE), jnp.float32)
    empty_key_gradient = jnp.zeros((TOKEN_COUNT, KEY_VALUE_HEADS, HEAD_SIZE), jnp.float32)

    def one_block(running, block_index):
        key_gradient_total, value_gradient_total = running
        first = block_index * KEYS_PER_TILE
        q_block = lax.dynamic_slice_in_dim(query_four, first, KEYS_PER_TILE, 0)
        d_block = lax.dynamic_slice_in_dim(output_grad_four, first, KEYS_PER_TILE, 0)
        q_pos = first + jnp.arange(KEYS_PER_TILE, dtype=jnp.int32)
        q_start = lax.dynamic_slice_in_dim(starts_all, first, KEYS_PER_TILE, 0)
        lowest = q_start[0] // KEYS_PER_TILE

        def key_slices(tile_index):
            k_first = tile_index * KEYS_PER_TILE
            key_tile = lax.dynamic_slice_in_dim(key_three, k_first, KEYS_PER_TILE, 0)
            value_tile = lax.dynamic_slice_in_dim(value_three, k_first, KEYS_PER_TILE, 0)
            k_pos = k_first + jnp.arange(KEYS_PER_TILE, dtype=jnp.int32)
            return k_first, key_tile, value_tile, k_pos

        def stats_tile(tile_index, sums_pair):
            weight_sums, weighted = sums_pair
            k_first, key_tile, value_tile, k_pos = key_slices(tile_index)
            bent, scores, visible, dots = score_tile(q_block, d_block, key_tile, value_tile, q_pos, q_start, k_pos)
            weights = jnp.where(visible, jnp.exp(scores), 0.0)
            return weight_sums + jnp.sum(weights, axis=-1), weighted + jnp.sum(weights * dots, axis=-1)

        weight_sums, weighted = lax.fori_loop(lowest, block_index + 1, stats_tile, (empty_row_stat, empty_row_stat))
        log_norm = jnp.log(weight_sums)
        row_dots = weighted / weight_sums

        def grad_tile(tile_index, accs):
            key_part, value_part, query_part = accs
            k_first, key_tile, value_tile, k_pos = key_slices(tile_index)
            bent, scores, visible, dots = score_tile(q_block, d_block, key_tile, value_tile, q_pos, q_start, k_pos)
            probability = jnp.where(visible, jnp.exp(scores - log_norm[..., None]), 0.0)
            prob_low = lax.optimization_barrier(probability.astype(jnp.bfloat16)).astype(jnp.float32)
            slope_grad = probability * (dots - row_dots[..., None]) * (1.0 - bent * bent)
            slope_low = lax.optimization_barrier(slope_grad.astype(jnp.bfloat16)).astype(jnp.float32)
            value_term = jnp.einsum("rngk,rngd->knd", prob_low, d_block.astype(jnp.float32))
            key_term = jnp.einsum("rngk,rngd->knd", slope_low, q_block.astype(jnp.float32))
            query_term = jnp.einsum("rngk,knd->rngd", slope_low, key_tile.astype(jnp.float32))
            old_keys = lax.dynamic_slice_in_dim(key_part, k_first, KEYS_PER_TILE, 0)
            old_values = lax.dynamic_slice_in_dim(value_part, k_first, KEYS_PER_TILE, 0)
            key_part = lax.dynamic_update_slice_in_dim(key_part, old_keys + key_term, k_first, 0)
            value_part = lax.dynamic_update_slice_in_dim(value_part, old_values + value_term, k_first, 0)
            return key_part, value_part, query_part + query_term

        key_gradient_total, value_gradient_total, query_block = lax.fori_loop(lowest, block_index + 1, grad_tile, (key_gradient_total, value_gradient_total, empty_query_gradient))
        return (key_gradient_total, value_gradient_total), query_block

    (key_gradient_total, value_gradient_total), query_all = lax.scan(one_block, (empty_key_gradient, empty_key_gradient), jnp.arange(blocks, dtype=jnp.int32))
    dq_home = (query_all.reshape(TOKEN_COUNT, QUERY_HEADS * HEAD_SIZE) * logit_scale).astype(jnp.bfloat16)
    key_gradient_home = (key_gradient_total * logit_scale).astype(jnp.bfloat16).reshape(TOKEN_COUNT, KEY_VALUE_HEADS * HEAD_SIZE)
    value_gradient_home = value_gradient_total.astype(jnp.bfloat16).reshape(TOKEN_COUNT, KEY_VALUE_HEADS * HEAD_SIZE)
    per_owner = TOK_DEV // N_CTX
    lists = send_order.reshape(N_CTX, N_CTX, per_owner)
    home_rows = jnp.transpose(lists, (1, 0, 2)) + (jnp.arange(N_CTX, dtype=jnp.int32) * TOK_DEV)[None, :, None]
    dq_owned = dq_home[home_rows.reshape(TOKEN_COUNT).astype(jnp.int32)]
    return dq_owned, key_gradient_home, value_gradient_home
```

```python
import functools
import math

import jax
import jax.numpy as jnp
from jax import lax
from jax.experimental import pallas as pl
from jax.experimental.pallas import tpu as pltpu
from jax.sharding import PartitionSpec as P

HEAD_SIZE = 128
SOFTCAP = 30
TOK = 128
ROWS_Y = 4
RING = 8
UNIT = 2 * TOK
SLOTS = 3 * RING
SUM_ROWS = 16
MESH = pl.DeviceIdType.MESH
F32 = jnp.float32
BF16 = jnp.bfloat16


def dot(a, b, contract=((1,), (0,))):
    return lax.dot_general(a, b, (contract, ((), ())), preferred_element_type=F32)


def send(src, dst, send_sem, recv_sem, target):
    return pltpu.make_async_remote_copy(
        src_ref=src,
        dst_ref=dst,
        send_sem=send_sem,
        recv_sem=recv_sem,
        device_id={"ctx": target},
        device_id_type=MESH,
    )


def travels(row, way, origin, hop, core):
    if row == 0:
        if way == 0:
            return (hop <= 4) & (origin + hop <= RING - 1)
        return (hop <= 3) & (origin <= 2)
    if row == 2:
        if way == 1:
            return (hop <= 4) & (origin - hop >= 0)
        return (hop <= 3) & (origin >= 5)
    return hop <= (4 - core if way == 0 else 3 + core)


def needed(row, origin, z):
    return (row == 1) | ((row == 0) & (origin <= z)) | ((row == 2) & (origin >= z))


def kernel(
    lengths,
    order,
    queries,
    cotangent,
    keys,
    values,
    dq_out,
    dk_out,
    dv_out,
    kv,
    exps,
    slopes,
    q_t,
    d_t,
    q_scaled,
    d_scaled,
    out_acc,
    dq_acc,
    low,
    inverse,
    row_dots,
    bounds,
    part,
    sib_out,
    sib_in,
    ring_out,
    ring_in,
    y_in,
    g_ring_send,
    g_ring_recv,
    g_sib_send,
    g_sib_recv,
    g_y_send,
    g_y_recv,
    r_ring_send,
    r_ring_recv,
    r_sib_send,
    r_sib_recv,
    r_y_send,
    r_y_recv,
):
    lanes = queries.shape[1]
    heads = lanes // HEAD_SIZE
    index = lax.axis_index("ctx")
    core = lax.rem(index, 2)
    z = lax.rem(lax.div(index, 2), RING)
    h = lax.div(index, 2 * RING)
    sibling = index + 1 - 2 * core
    above = 2 * RING * h + 2 * lax.rem(z + 1, RING) + core
    below = 2 * RING * h + 2 * lax.rem(z + RING - 1, RING) + core
    toward = (above, below)
    scale = 1.0 / math.sqrt(HEAD_SIZE)

    barrier = pltpu.get_barrier_semaphore()
    for partner in (sibling, above, below):
        pl.semaphore_signal(barrier, inc=1, device_id={"ctx": partner}, device_id_type=MESH)
    for step in (-2, -1, 1, 2):

        @pl.when((h + step >= 0) & (h + step < ROWS_Y))
        def _():
            pl.semaphore_signal(
                barrier,
                inc=1,
                device_id={"ctx": index + step * 2 * RING},
                device_id_type=MESH,
            )

    own = kv.at[z, core]
    own[0] = keys[...]
    own[1] = values[...]
    pl.semaphore_wait(barrier, jnp.where((h == 1) | (h == 2), 6, 5))

    def place(row, way, distance):
        origin = lax.rem(z + RING + (distance if way else -distance), RING)
        return origin, row * RING + origin

    def gather_ring(row, way, slot):
        unit = kv.at[slot, core]
        return send(unit, unit, g_ring_send.at[way, slot], g_ring_recv.at[slot], toward[way])

    def gather_sib(slot, side):
        unit = kv.at[slot, side]
        return send(unit, unit, g_sib_send.at[slot], g_sib_recv.at[slot], sibling)

    def gather_y(step):
        return send(
            kv.at[z, core],
            kv.at[step * RING + z, core],
            g_y_send.at[step - 1],
            g_y_recv.at[step - 1],
            lax.rem(index + step * 2 * RING, 2 * RING * ROWS_Y),
        )

    def reduce_sib(slot):
        return send(sib_out.at[slot], sib_in.at[slot], r_sib_send.at[slot], r_sib_recv.at[slot], sibling)

    def reduce_ring(way, slot):
        return send(
            ring_out.at[slot],
            ring_in.at[way, slot],
            r_ring_send.at[slot],
            r_ring_recv.at[way, slot],
            toward[1 - way],
        )

    def reduce_y(step):
        return send(
            ring_out.at[step * RING + z],
            y_in.at[step - 1],
            r_y_send.at[step - 1],
            r_y_recv.at[step - 1],
            lax.rem(index + (ROWS_Y - step) * 2 * RING, 2 * RING * ROWS_Y),
        )

    for step in (1, 2):

        @pl.when(h + step < ROWS_Y)
        def _():
            gather_y(step).start()

    def arrivals(t):
        for row in range(3):
            distance = t - row

            @pl.when((distance == 0) & (h >= row))
            def _():
                if row:
                    gather_y(row).wait_recv()
                slot = row * RING + z
                for way in (0, 1):

                    @pl.when(travels(row, way, z, 1, core))
                    def _():
                        gather_ring(row, way, slot).start()

                gather_sib(slot, core).start()

            for way in (0, 1):
                origin, slot = place(row, way, distance)

                @pl.when(
                    (distance >= 1)
                    & (distance <= 4)
                    & (h >= row)
                    & travels(row, way, origin, distance, core)
                )
                def _():
                    gather_ring(row, way, slot).wait_recv()

                    @pl.when(travels(row, way, origin, distance + 1, core))
                    def _():
                        gather_ring(row, way, slot).start()

                    @pl.when(needed(row, origin, z))
                    def _():
                        gather_sib(slot, core).start()

    arrivals(0)

    for n in range(heads):
        cols = slice(n * HEAD_SIZE, (n + 1) * HEAD_SIZE)
        q_t[:, cols] = queries[:, cols].astype(F32).T.astype(BF16)
        d_t[:, cols] = cotangent[:, cols].astype(F32).T.astype(BF16)
    out_acc[...] = jnp.zeros_like(out_acc)
    dq_acc[...] = jnp.zeros_like(dq_acc)
    position = index * TOK + lax.broadcasted_iota(jnp.int32, (8, TOK), 1)
    start = jnp.zeros((8, TOK), jnp.int32)
    first = jnp.int32(0)
    for doc in range(lengths.shape[0]):
        start = jnp.where(position >= first, jnp.maximum(start, first), start)
        first = first + lengths[doc]
    bounds[0] = start
    bounds[1] = position

    def slot_of(row, way, distance):
        origin = lax.rem(z + RING + (2 * way - 1) * distance, RING)
        valid = (
            (h >= row)
            & (distance >= 0)
            & (distance <= 4)
            & needed(row, origin, z)
            & ((way == 0) | ((distance != 0) & (distance != 4)))
        )
        return origin, row * RING + origin, valid

    pairs = [slice(p * 2 * HEAD_SIZE, min((p + 1) * 2 * HEAD_SIZE, lanes)) for p in range((heads + 1) // 2)]

    def statistics(row, origin, slot):
        gather_sib(slot, 1 - core).wait_recv()
        key = kv[slot, :, 0].reshape(UNIT, HEAD_SIZE)
        value = kv[slot, :, 1].reshape(UNIT, HEAD_SIZE)
        value_t = jnp.concatenate(
            [value.astype(F32).T.astype(BF16), jnp.ones((SUM_ROWS, UNIT), BF16)], axis=0
        )
        key_at = ((h - row) * RING + origin) * UNIT + lax.broadcasted_iota(jnp.int32, (UNIT, TOK), 0)
        visible = (key_at >= bounds[0, :1]) & (key_at <= bounds[1, :1])
        for cols in pairs:
            wide = (cols.stop - cols.start) // TOK
            seen = jnp.concatenate([visible] * wide, axis=1) if wide > 1 else visible
            raw = dot(key, q_t[:, cols])
            bent = jnp.tanh(raw * (scale / SOFTCAP))
            weight = jnp.where(seen, jnp.exp2(bent * (SOFTCAP * math.log2(math.e))), 0.0)
            slopes[slot, :, cols] = weight - weight * bent * bent
            weight_low = weight.astype(BF16)
            exps[slot, :, cols] = weight_low
            out_acc[:, cols] += dot(value_t, weight_low)

    def gather_step(t, carry):
        @pl.when(t < 7)
        def _():
            arrivals(t)

        def one(q, carry):
            row, way = lax.div(q, 2), lax.rem(q, 2)
            origin, slot, valid = slot_of(row, way, t - 1 - row)

            @pl.when(valid)
            def _():
                statistics(row, origin, slot)

            return carry

        return lax.fori_loop(0, 6, one, carry)

    lax.fori_loop(1, 8, gather_step, 0)

    inverse_sum = 1.0 / out_acc[HEAD_SIZE : HEAD_SIZE + 8, :]
    inverse[...] = inverse_sum
    for n in range(heads):
        cols = slice(n * HEAD_SIZE, (n + 1) * HEAD_SIZE)
        inv = inverse_sum[:1, cols]
        d_n = d_t[:, cols].astype(F32)
        dots = jnp.sum(out_acc[:HEAD_SIZE, cols] * d_n, axis=0, keepdims=True) * inv
        row_dots[:, cols] = jnp.broadcast_to(dots, (8, HEAD_SIZE))
        d_scaled[cols, :] = (d_n * inv).T.astype(BF16)
        q_scaled[cols, :] = (q_t[:, cols].astype(F32) * inv).T.astype(BF16)

    def gradients(slot):
        key = kv[slot, :, 0].reshape(UNIT, HEAD_SIZE)
        value = kv[slot, :, 1].reshape(UNIT, HEAD_SIZE)
        key_t = key.astype(F32).T.astype(BF16)
        for cols in pairs:
            dots = dot(value, d_t[:, cols]) - row_dots[:1, cols]
            slope = (slopes[slot, :, cols] * dots).astype(BF16)
            low[:, cols] = slope
            dq_acc[:, cols] += dot(key_t, slope)
        key_part = dot(low[...], q_scaled[...])
        value_part = dot(exps[slot], d_scaled[...])
        for side in (0, 1):
            rows = slice(side * TOK, (side + 1) * TOK)

            @pl.when(core == side)
            def _():
                part[slot, 0] = key_part[rows]
                part[slot, 1] = value_part[rows]

            @pl.when(core != side)
            def _():
                sib_out[slot, 0] = key_part[rows].astype(BF16)
                sib_out[slot, 1] = value_part[rows].astype(BF16)

        reduce_sib(slot).start()

    def combine(u):
        for row in (2, 1, 0):
            distance = 5 - u + (2 - row)
            for way in (0, 1):
                origin, slot = place(row, way, distance)

                @pl.when(
                    (distance >= 1)
                    & (distance <= 4)
                    & (h >= row)
                    & travels(row, way, origin, distance, core)
                )
                def _():
                    @pl.when(needed(row, origin, z))
                    def _():
                        reduce_sib(slot).wait_recv()
                        part[slot] = part[slot] + sib_in[slot].astype(F32)

                    @pl.when(jnp.logical_not(needed(row, origin, z)))
                    def _():
                        part[slot] = jnp.zeros(part.shape[1:], F32)

                    @pl.when(travels(row, way, origin, distance + 1, core))
                    def _():
                        reduce_ring(way, slot).wait_recv()
                        part[slot] = part[slot] + ring_in[way, slot].astype(F32)

                    ring_out[slot] = part[slot].astype(BF16)
                    reduce_ring(way, slot).start()

            @pl.when((distance == 0) & (h >= row))
            def _():
                slot = row * RING + z
                reduce_sib(slot).wait_recv()
                part[slot] = part[slot] + sib_in[slot].astype(F32)
                for way in (0, 1):

                    @pl.when(travels(row, way, z, 1, core))
                    def _():
                        reduce_ring(way, slot).wait_recv()
                        part[slot] = part[slot] + ring_in[way, slot].astype(F32)

                if row:
                    ring_out[slot] = part[slot].astype(BF16)
                    reduce_y(row).start()

    def reduce_step(u, carry):
        def one(q, carry):
            row, way = 2 - lax.div(q, 2), lax.rem(q, 2)
            _, slot, valid = slot_of(row, way, 6 - u - row)

            @pl.when(valid)
            def _():
                gradients(slot)

            return carry

        carry = lax.fori_loop(0, 6, one, carry)
        combine(u)
        return carry

    lax.fori_loop(0, 8, reduce_step, 0)

    picked = (lax.broadcasted_iota(jnp.int32, (TOK, TOK), 0) == order[...]).astype(F32).T.astype(BF16)
    for n in range(heads):
        cols = slice(n * HEAD_SIZE, (n + 1) * HEAD_SIZE)
        grad_t = (dq_acc[:, cols] * (inverse[:1, cols] * scale)).astype(BF16)
        dq_out[:, cols] = dot(picked, grad_t, ((1,), (1,))).astype(BF16)

    for step in (1, 2):

        @pl.when(h + step < ROWS_Y)
        def _():
            reduce_y(step).wait_recv()
            part[z] = part[z] + y_in[step - 1].astype(F32)

    dk_out[...] = (part[z, 0] * scale).astype(BF16)
    dv_out[...] = part[z, 1].astype(BF16)

    for step in (1, 2):

        @pl.when(h + step < ROWS_Y)
        def _():
            gather_y(step).wait_send()

        @pl.when(h >= step)
        def _():
            reduce_y(step).wait_send()

    def drain(distance, carry):
        for row in range(3):
            for way in (0, 1):
                origin, slot = place(row, way, distance)

                @pl.when((h >= row) & travels(row, way, origin, distance + 1, core))
                def _():
                    gather_ring(row, way, slot).wait_send()

                @pl.when(
                    (distance >= 1) & (h >= row) & travels(row, way, origin, distance, core)
                )
                def _():
                    reduce_ring(way, slot).wait_send()

                _, _, valid = slot_of(row, way, distance)

                @pl.when(valid)
                def _():
                    gather_sib(slot, core).wait_send()
                    reduce_sib(slot).wait_send()

        return carry

    lax.fori_loop(0, 5, drain, 0)


def run_kernel(queries, cotangent, keys, values, lengths, order):
    lanes = queries.shape[1]
    vmem = pl.BlockSpec(memory_space=pltpu.VMEM)
    block = (2, TOK, HEAD_SIZE)
    dma = pltpu.SemaphoreType.DMA
    return pl.pallas_call(
        kernel,
        out_shape=(
            jax.ShapeDtypeStruct((TOK, lanes), BF16),
            jax.ShapeDtypeStruct((TOK, HEAD_SIZE), BF16),
            jax.ShapeDtypeStruct((TOK, HEAD_SIZE), BF16),
        ),
        in_specs=[pl.BlockSpec(memory_space=pltpu.SMEM)] + [vmem] * 5,
        out_specs=(vmem, vmem, vmem),
        scratch_shapes=[
            pltpu.VMEM((SLOTS, 2) + block, BF16),
            pltpu.VMEM((SLOTS, UNIT, lanes), BF16),
            pltpu.VMEM((SLOTS, UNIT, lanes), F32),
            pltpu.VMEM((HEAD_SIZE, lanes), BF16),
            pltpu.VMEM((HEAD_SIZE, lanes), BF16),
            pltpu.VMEM((lanes, HEAD_SIZE), BF16),
            pltpu.VMEM((lanes, HEAD_SIZE), BF16),
            pltpu.VMEM((HEAD_SIZE + SUM_ROWS, lanes), F32),
            pltpu.VMEM((HEAD_SIZE, lanes), F32),
            pltpu.VMEM((UNIT, lanes), BF16),
            pltpu.VMEM((8, lanes), F32),
            pltpu.VMEM((8, lanes), F32),
            pltpu.VMEM((2, 8, TOK), jnp.int32),
            pltpu.VMEM((SLOTS,) + block, F32),
            pltpu.VMEM((SLOTS,) + block, BF16),
            pltpu.VMEM((SLOTS,) + block, BF16),
            pltpu.VMEM((SLOTS,) + block, BF16),
            pltpu.VMEM((2, SLOTS) + block, BF16),
            pltpu.VMEM((2,) + block, BF16),
            dma((2, SLOTS)),
            dma((SLOTS,)),
            dma((SLOTS,)),
            dma((SLOTS,)),
            dma((2,)),
            dma((2,)),
            dma((SLOTS,)),
            dma((2, SLOTS)),
            dma((SLOTS,)),
            dma((SLOTS,)),
            dma((2,)),
            dma((2,)),
        ],
        compiler_params=pltpu.CompilerParams(
            collective_id=0, has_side_effects=True, vmem_limit_bytes=58 * 1024 * 1024
        ),
        name="attention_backward",
    )(lengths, order, queries, cotangent, keys, values)


def on_device(queries, keys, values, output_cotangent, lengths, send_order):
    rows, lanes = queries.shape
    dq, dk, dv = run_kernel(queries, output_cotangent, keys, values, lengths, send_order)
    owners = lax.axis_size("ctx")
    moved = dq.reshape(owners, rows // owners, lanes)
    dq_owned = lax.all_to_all(moved, "ctx", split_axis=0, concat_axis=0, tiled=True)
    return dq_owned.reshape(rows, lanes), dk, dv


def solution(mesh):
    return jax.shard_map(
        on_device,
        mesh=mesh,
        in_specs=(
            P("ctx", "head"),
            P("ctx", "head"),
            P("ctx", "head"),
            P("ctx", "head"),
            P(),
            P("ctx", None),
        ),
        out_specs=(P("ctx", "head"), P("ctx", "head"), P("ctx", "head")),
        check_vma=False,
    )
```

```python
import functools
import math

import jax
import jax.numpy as jnp
from jax import lax
from jax.experimental import pallas as pl
from jax.experimental.pallas import tpu as pltpu
from jax.sharding import PartitionSpec as P

HEAD_SIZE = 128
SOFTCAP = 30
TOK = 128
ROWS_Y = 4
RING = 8
UNIT = 2 * TOK
SLOTS = 3 * RING
SUM_ROWS = 16
HELD = 17
PAD = 8
GATHER_ORDER = ((0, 0), (1, 0), (0, 1), (2, 0), (1, 1), (2, 1), (0, 2), (1, 2), (2, 2))
REDUCE_ORDER = ((2, 2), (1, 2), (0, 2), (2, 1), (1, 1), (0, 1), (2, 0), (1, 0), (0, 0))
STAGES = ((), (2, -2, 1, -1), (3, -3, 4, -4))
PORT = {1: 0, 2: 1, -1: 2, -2: 3, 3: 4, 4: 5, -3: 6, -4: 7}
MESH = pl.DeviceIdType.MESH
F32 = jnp.float32
BF16 = jnp.bfloat16


def dot(a, b, contract=((1,), (0,))):
    return lax.dot_general(a, b, (contract, ((), ())), preferred_element_type=F32)


def send(src, dst, send_sem, recv_sem, target):
    return pltpu.make_async_remote_copy(
        src_ref=src,
        dst_ref=dst,
        send_sem=send_sem,
        recv_sem=recv_sem,
        device_id={"ctx": target},
        device_id_type=MESH,
    )


def needed(row, origin, z):
    return (row == 1) | ((row == 0) & (origin <= z)) | ((row == 2) & (origin >= z))


def reaches(row, origin, shift, core):
    z = lax.rem(origin + shift + RING, RING)
    if abs(shift) == 4:
        if row == 1:
            return core == (0 if shift > 0 else 1)
        return needed(row, origin, z) & ((row == 0) == (shift > 0))
    wanted = needed(row, origin, z)
    if abs(shift) == 2:
        for further in (3, 4):
            wanted = wanted | reaches(row, origin, further if shift > 0 else -further, core)
    return wanted


def pick(index, table):
    value = jnp.int32(table[0])
    for i in range(1, len(table)):
        value = jnp.where(index == i, table[i], value)
    return value


def kernel(
    lengths,
    order,
    queries,
    cotangent,
    keys,
    values,
    dq_out,
    dk_out,
    dv_out,
    kv,
    exps,
    slopes,
    q_t,
    d_t,
    q_rows,
    d_rows,
    out_acc,
    dq_acc,
    low_slope,
    low_prob,
    inverse,
    row_dots,
    bounds,
    spread,
    part,
    sib_out,
    sib_in,
    ring_out,
    ring_in,
    y_in,
    rows_out,
    rows_in,
    g_ring_send,
    g_ring_recv,
    g_sib_send,
    g_sib_recv,
    g_y_send,
    g_y_recv,
    r_ring_send,
    r_ring_recv,
    r_sib_send,
    r_sib_recv,
    r_y_send,
    r_y_recv,
    rows_send,
    rows_recv,
    ready,
):
    lanes = queries.shape[1]
    heads = lanes // HEAD_SIZE
    devices = 2 * RING * ROWS_Y
    index = lax.axis_index("ctx")
    core = lax.rem(index, 2)
    z = lax.rem(lax.div(index, 2), RING)
    h = lax.div(index, 2 * RING)
    sibling = index + 1 - 2 * core
    scale = 1.0 / math.sqrt(HEAD_SIZE)

    def along(place):
        return 2 * RING * h + 2 * lax.rem(place + RING, RING) + core

    barrier = pltpu.get_barrier_semaphore()
    ring_mates = [along(z + step) for step in range(1, RING)]
    column_mates = [
        lax.rem(index - core + 2 * RING * step + lax.rem(core + side, 2), devices)
        for step in range(ROWS_Y)
        for side in (0, 1)
        if step or side
    ]
    for mate in ring_mates + column_mates:
        pl.semaphore_signal(barrier, inc=1, device_id={"ctx": mate}, device_id_type=MESH)

    own = kv.at[z, core]
    own[0] = keys[...]
    own[1] = values[...]
    pl.semaphore_wait(barrier, len(ring_mates + column_mates))

    def gather_ring(row, origin, shift):
        unit = kv.at[row * RING + origin, core]
        return send(
            unit,
            unit,
            g_ring_send.at[row, PORT[shift]],
            g_ring_recv.at[row * RING + origin],
            along(origin + shift),
        )

    def gather_sib(slot, side):
        unit = kv.at[slot, side]
        return send(unit, unit, g_sib_send.at[slot], g_sib_recv.at[slot], sibling)

    def gather_y(step):
        return send(
            kv.at[z, core],
            kv.at[step * RING + z, core],
            g_y_send.at[step - 1],
            g_y_recv.at[step - 1],
            lax.rem(index + step * 2 * RING, devices),
        )

    def reduce_sib(slot):
        return send(sib_out.at[slot], sib_in.at[slot], r_sib_send.at[slot], r_sib_recv.at[slot], sibling)

    def reduce_ring(row, origin, shift):
        stop = 0 if abs(shift) <= 2 else (2 if shift > 0 else -2)
        return send(
            ring_out.at[row * RING + origin],
            ring_in.at[row, PORT[shift]],
            r_ring_send.at[row * RING + origin],
            r_ring_recv.at[row, PORT[shift]],
            along(origin + stop),
        )

    def reduce_y(step):
        return send(
            ring_out.at[step * RING + z],
            y_in.at[step - 1],
            r_y_send.at[step - 1],
            r_y_recv.at[step - 1],
            lax.rem(index + (ROWS_Y - step) * 2 * RING, devices),
        )

    for step in (1, 2):

        @pl.when(h + step < ROWS_Y)
        def _():
            gather_y(step).start()

    def origin_of(shift):
        return lax.rem(z - shift + RING, RING)

    def further_of(shift):
        if abs(shift) != 2:
            return ()
        return (3, 4) if shift > 0 else (-3, -4)

    def arrive(row, stage):
        if stage == 0:
            if row:
                gather_y(row).wait_recv()
            for shift in (2, -2, 1, -1):

                @pl.when(reaches(row, z, shift, core))
                def _():
                    gather_ring(row, z, shift).start()

            gather_sib(row * RING + z, core).start()
        for shift in STAGES[stage]:
            origin = origin_of(shift)

            @pl.when(reaches(row, origin, shift, core))
            def _():
                gather_ring(row, origin, shift).wait_recv()
                for further in further_of(shift):

                    @pl.when(reaches(row, origin, further, core))
                    def _():
                        gather_ring(row, origin, further).start()

                @pl.when(needed(row, origin, z))
                def _():
                    gather_sib(row * RING + origin, core).start()

    arrive(*GATHER_ORDER[0])
    for mate in column_mates:
        pl.semaphore_signal(ready, inc=1, device_id={"ctx": mate}, device_id_type=MESH)

    for n in range(heads):
        cols = slice(n * HEAD_SIZE, (n + 1) * HEAD_SIZE)
        q_t[:, cols] = queries[:, cols].astype(F32).T.astype(BF16)
        d_t[:, cols] = cotangent[:, cols].astype(F32).T.astype(BF16)
        q_rows[cols, :] = queries[:, cols]
        d_rows[cols, :] = cotangent[:, cols]
    out_acc[...] = jnp.zeros_like(out_acc)
    dq_acc[...] = jnp.zeros_like(dq_acc)
    position = index * TOK + lax.broadcasted_iota(jnp.int32, (8, TOK), 1)
    start = jnp.zeros((8, TOK), jnp.int32)
    first = jnp.int32(0)
    for doc in range(lengths.shape[0]):
        start = jnp.where(position >= first, jnp.maximum(start, first), start)
        first = first + lengths[doc]
    bounds[0] = start
    bounds[1] = position

    picked = (lax.broadcasted_iota(jnp.int32, (TOK, TOK), 0) == order[...]).astype(F32).T.astype(BF16)
    target = lax.broadcasted_iota(jnp.int32, (TOK * PAD, TOK), 0)
    source = PAD * lax.broadcasted_iota(jnp.int32, (TOK * PAD, TOK), 1)
    for n in range(heads):
        place = (target == source + n).astype(F32).astype(BF16)
        spread[:, n * HEAD_SIZE : (n + 1) * HEAD_SIZE] = dot(place, picked).astype(BF16)

    def member(row, stage, i):
        distance = jnp.where(stage == 0, 0, 2 * stage - 1 + lax.div(i, 2))
        origin = lax.rem(z + RING + (2 * lax.rem(i, 2) - 1) * distance, RING)
        count = jnp.where(stage == 0, 1, jnp.where(stage == 1, 4, 3))
        valid = (h >= row) & needed(row, origin, z) & (i < count)
        kept = jnp.where(row == 1, RING + origin, jnp.where((row == 2) & (origin == z), 2 * RING, origin))
        return origin, row * RING + origin, kept, valid

    def statistics(row, origin, slot, kept):
        gather_sib(slot, 1 - core).wait_recv()
        key = kv[slot, :, 0].reshape(UNIT, HEAD_SIZE)
        value = kv[slot, :, 1].reshape(UNIT, HEAD_SIZE)
        value_t = jnp.concatenate(
            [value.astype(F32).T.astype(BF16), jnp.ones((SUM_ROWS, UNIT), BF16)], axis=0
        )
        key_at = ((h - row) * RING + origin) * UNIT + lax.broadcasted_iota(jnp.int32, (UNIT, TOK), 0)
        visible = (key_at >= bounds[0, :1]) & (key_at <= bounds[1, :1])
        seen = jnp.concatenate([visible] * heads, axis=1)
        bent = jnp.tanh(dot(key, q_t[...]) * (scale / SOFTCAP))
        weight = jnp.where(seen, jnp.exp2(bent * (SOFTCAP * math.log2(math.e))), 0.0)
        exps[kept] = weight
        slopes[kept] = weight - weight * bent * bent
        out_acc[...] += dot(value_t, weight.astype(BF16))

    def gather_step(g, carry):
        for i in range(1, len(GATHER_ORDER)):

            @pl.when((g == i) & (h >= GATHER_ORDER[i][0]))
            def _():
                arrive(*GATHER_ORDER[i])

        row = pick(g - 1, [r for r, _ in GATHER_ORDER])
        stage = pick(g - 1, [s for _, s in GATHER_ORDER])

        def one(i, carry):
            origin, slot, kept, valid = member(row, stage, i)

            @pl.when(valid)
            def _():
                statistics(row, origin, slot, kept)

            return carry

        return lax.fori_loop(0, 4, one, carry)

    lax.fori_loop(1, len(GATHER_ORDER) + 1, gather_step, 0)

    inverse_sum = 1.0 / out_acc[HEAD_SIZE : HEAD_SIZE + 8, :]
    inverse[...] = inverse_sum
    dots = jnp.sum(out_acc[:HEAD_SIZE, :] * d_t[...].astype(F32), axis=0, keepdims=True)
    row_dots[...] = dots * inverse_sum

    def gradients(slot, kept):
        key = kv[slot, :, 0].reshape(UNIT, HEAD_SIZE)
        value = kv[slot, :, 1].reshape(UNIT, HEAD_SIZE)
        key_t = key.astype(F32).T.astype(BF16)
        inv = inverse[:1, :]
        dots = (dot(value, d_t[...]) - row_dots[:1, :]) * inv
        slope = (slopes[kept] * dots).astype(BF16)
        low_slope[...] = slope
        low_prob[...] = (exps[kept] * inv).astype(BF16)
        dq_acc[...] += dot(key_t, slope)
        key_part = dot(low_slope[...], q_rows[...])
        value_part = dot(low_prob[...], d_rows[...])
        for side in (0, 1):
            rows = slice(side * TOK, (side + 1) * TOK)

            @pl.when(core == side)
            def _():
                part[slot, 0] = key_part[rows]
                part[slot, 1] = value_part[rows]

            @pl.when(core != side)
            def _():
                sib_out[slot, 0] = key_part[rows].astype(BF16)
                sib_out[slot, 1] = value_part[rows].astype(BF16)

        reduce_sib(slot).start()

    def combine(row, stage):
        if stage == 0:
            slot = row * RING + z
            reduce_sib(slot).wait_recv()
            part[slot] = part[slot] + sib_in[slot].astype(F32)
            for shift in (1, -1, 2, -2):

                @pl.when(reaches(row, z, shift, core))
                def _():
                    reduce_ring(row, z, shift).wait_recv()
                    part[slot] = part[slot] + ring_in[row, PORT[shift]].astype(F32)

            if row:
                ring_out[slot] = part[slot].astype(BF16)
                reduce_y(row).start()
        for shift in STAGES[stage]:
            origin = origin_of(shift)
            slot = row * RING + origin

            @pl.when(reaches(row, origin, shift, core))
            def _():
                if stage == 1:

                    @pl.when(jnp.logical_not(needed(row, origin, z)))
                    def _():
                        part[slot] = jnp.zeros(part.shape[1:], F32)

                @pl.when(needed(row, origin, z))
                def _():
                    reduce_sib(slot).wait_recv()
                    part[slot] = part[slot] + sib_in[slot].astype(F32)

                for further in further_of(shift):

                    @pl.when(reaches(row, origin, further, core))
                    def _():
                        reduce_ring(row, origin, further).wait_recv()
                        part[slot] = part[slot] + ring_in[row, PORT[further]].astype(F32)

                ring_out[slot] = part[slot].astype(BF16)
                reduce_ring(row, origin, shift).start()

    def reduce_step(g, carry):
        row = pick(g, [r for r, _ in REDUCE_ORDER])
        stage = pick(g, [s for _, s in REDUCE_ORDER])

        def one(i, carry):
            _, slot, kept, valid = member(row, stage, i)

            @pl.when(valid)
            def _():
                gradients(slot, kept)

            return carry

        carry = lax.fori_loop(0, 4, one, carry)
        for i in range(len(REDUCE_ORDER) - 1):

            @pl.when((g == i + 1) & (h >= REDUCE_ORDER[i][0]))
            def _():
                combine(*REDUCE_ORDER[i])

        return carry

    lax.fori_loop(0, len(REDUCE_ORDER), reduce_step, 0)

    grad_t = (dq_acc[...] * scale).astype(BF16)
    moved = dot(spread[...], grad_t, ((1,), (1,))).astype(BF16)
    rows_out[...] = moved.reshape(rows_out.shape)

    pl.semaphore_wait(ready, len(column_mates))

    def rows_to(step, carry):
        owner = lax.rem(index + step, devices)
        send(rows_out.at[owner], rows_in.at[index], rows_send, rows_recv, owner).start()
        return carry

    lax.fori_loop(1, devices, rows_to, 0)
    rows_in[index] = rows_out[index]

    combine(*REDUCE_ORDER[-1])
    for step in (1, 2):

        @pl.when(h + step < ROWS_Y)
        def _():
            reduce_y(step).wait_recv()
            part[z] = part[z] + y_in[step - 1].astype(F32)

    dk_out[...] = (part[z, 0] * scale).astype(BF16)
    dv_out[...] = part[z, 1].astype(BF16)

    for step in (1, 2):

        @pl.when(h + step < ROWS_Y)
        def _():
            gather_y(step).wait_send()

        @pl.when(h >= step)
        def _():
            reduce_y(step).wait_send()

    for row in range(3):

        @pl.when(h >= row)
        def _():
            gather_sib(row * RING + z, core).wait_send()
            reduce_sib(row * RING + z).wait_send()
            for shift in PORT:
                origin = origin_of(shift)
                if abs(shift) <= 2:

                    @pl.when(reaches(row, z, shift, core))
                    def _():
                        gather_ring(row, z, shift).wait_send()

                for further in further_of(shift):

                    @pl.when(reaches(row, origin, further, core))
                    def _():
                        gather_ring(row, origin, further).wait_send()

                @pl.when(reaches(row, origin, shift, core))
                def _():
                    reduce_ring(row, origin, shift).wait_send()

                    @pl.when(needed(row, origin, z))
                    def _():
                        gather_sib(row * RING + origin, core).wait_send()
                        reduce_sib(row * RING + origin).wait_send()

    others = pl.ds(0, devices - 1)
    everyone = send(rows_out.at[others], rows_in.at[others], rows_send, rows_recv, sibling)
    everyone.wait_recv()
    everyone.wait_send()
    dq_out[...] = rows_in[...]


def run_kernel(queries, cotangent, keys, values, lengths, order):
    lanes = queries.shape[1]
    devices = lax.axis_size("ctx")
    vmem = pl.BlockSpec(memory_space=pltpu.VMEM)
    block = (2, TOK, HEAD_SIZE)
    travelling = (devices, TOK // devices * PAD, HEAD_SIZE)
    dma = pltpu.SemaphoreType.DMA
    return pl.pallas_call(
        kernel,
        out_shape=(
            jax.ShapeDtypeStruct(travelling, BF16),
            jax.ShapeDtypeStruct((TOK, HEAD_SIZE), BF16),
            jax.ShapeDtypeStruct((TOK, HEAD_SIZE), BF16),
        ),
        in_specs=[pl.BlockSpec(memory_space=pltpu.SMEM)] + [vmem] * 5,
        out_specs=(vmem, vmem, vmem),
        scratch_shapes=[
            pltpu.VMEM((SLOTS, 2) + block, BF16),
            pltpu.VMEM((HELD, UNIT, lanes), F32),
            pltpu.VMEM((HELD, UNIT, lanes), F32),
            pltpu.VMEM((HEAD_SIZE, lanes), BF16),
            pltpu.VMEM((HEAD_SIZE, lanes), BF16),
            pltpu.VMEM((lanes, HEAD_SIZE), BF16),
            pltpu.VMEM((lanes, HEAD_SIZE), BF16),
            pltpu.VMEM((HEAD_SIZE + SUM_ROWS, lanes), F32),
            pltpu.VMEM((HEAD_SIZE, lanes), F32),
            pltpu.VMEM((UNIT, lanes), BF16),
            pltpu.VMEM((UNIT, lanes), BF16),
            pltpu.VMEM((8, lanes), F32),
            pltpu.VMEM((8, lanes), F32),
            pltpu.VMEM((2, 8, TOK), jnp.int32),
            pltpu.VMEM((TOK * PAD, lanes), BF16),
            pltpu.VMEM((SLOTS,) + block, F32),
            pltpu.VMEM((SLOTS,) + block, BF16),
            pltpu.VMEM((SLOTS,) + block, BF16),
            pltpu.VMEM((SLOTS,) + block, BF16),
            pltpu.VMEM((3, len(PORT)) + block, BF16),
            pltpu.VMEM((2,) + block, BF16),
            pltpu.VMEM(travelling, BF16),
            pltpu.VMEM(travelling, BF16),
            dma((3, len(PORT))),
            dma((SLOTS,)),
            dma((SLOTS,)),
            dma((SLOTS,)),
            dma((2,)),
            dma((2,)),
            dma((SLOTS,)),
            dma((3, len(PORT))),
            dma((SLOTS,)),
            dma((SLOTS,)),
            dma((2,)),
            dma((2,)),
            dma,
            dma,
            pltpu.SemaphoreType.REGULAR,
        ],
        compiler_params=pltpu.CompilerParams(
            collective_id=0, has_side_effects=True, vmem_limit_bytes=58 * 1024 * 1024
        ),
        name="attention_backward",
    )(lengths, order, queries, cotangent, keys, values)


def on_device(queries, keys, values, output_cotangent, lengths, send_order):
    rows, lanes = queries.shape
    moved, dk, dv = run_kernel(queries, output_cotangent, keys, values, lengths, send_order)
    dq_owned = moved.reshape(rows, PAD, HEAD_SIZE)[:, : lanes // HEAD_SIZE]
    return dq_owned.reshape(rows, lanes), dk, dv


def solution(mesh):
    return jax.shard_map(
        on_device,
        mesh=mesh,
        in_specs=(
            P("ctx", "head"),
            P("ctx", "head"),
            P("ctx", "head"),
            P("ctx", "head"),
            P(),
            P("ctx", None),
        ),
        out_specs=(P("ctx", "head"), P("ctx", "head"), P("ctx", "head")),
        check_vma=False,
    )
```

```python
import functools
import math

import jax
import jax.numpy as jnp
from jax import lax
from jax.experimental import pallas as pl
from jax.experimental.pallas import tpu as pltpu
from jax.sharding import PartitionSpec as P

HEAD_SIZE = 128
SOFTCAP = 30
TOK = 128
ROWS_Y = 4
RING = 8
SLOTS = 3 * RING
SUM_ROWS = 16
HELD = 17
PAD = 8
GATHER_ORDER = (
    (0, 0), (1, 0), (0, 2), (2, 0), (1, 2), (0, 1), (2, 2), (1, 1), (2, 1), (0, 3), (1, 3), (0, 4), (1, 4), (2, 3), (2, 4)
)
REDUCE_ORDER = (
    (2, 4), (2, 3), (1, 4), (1, 3), (0, 4), (0, 3), (2, 1), (1, 1), (2, 2), (1, 2), (0, 1), (2, 0), (0, 2), (1, 0), (0, 0)
)
PORT = {1: 0, 2: 1, -1: 2, -2: 3, 3: 4, 4: 5, -3: 6, -4: 7}
MESH = pl.DeviceIdType.MESH
F32 = jnp.float32
BF16 = jnp.bfloat16


def dot(a, b, contract=((1,), (0,))):
    return lax.dot_general(a, b, (contract, ((), ())), preferred_element_type=F32)


def send(src, dst, send_sem, recv_sem, target):
    return pltpu.make_async_remote_copy(
        src_ref=src,
        dst_ref=dst,
        send_sem=send_sem,
        recv_sem=recv_sem,
        device_id={"ctx": target},
        device_id_type=MESH,
    )


def needed(row, origin, z):
    return (row == 1) | ((row == 0) & (origin <= z)) | ((row == 2) & (origin >= z))


def reaches(row, origin, shift, core):
    z = lax.rem(origin + shift + RING, RING)
    if abs(shift) == 4:
        if row == 1:
            return core == (0 if shift > 0 else 1)
        return needed(row, origin, z) & ((row == 0) == (shift > 0))
    wanted = needed(row, origin, z)
    if abs(shift) == 2:
        for further in (3, 4):
            wanted = wanted | reaches(row, origin, further if shift > 0 else -further, core)
    return wanted


def pick(index, table):
    value = jnp.int32(table[0])
    for i in range(1, len(table)):
        value = jnp.where(index == i, table[i], value)
    return value


def kernel(
    lengths,
    order,
    queries,
    cotangent,
    keys,
    values,
    dq_out,
    dk_out,
    dv_out,
    kv,
    exps,
    slopes,
    q_t,
    d_t,
    q_rows,
    d_rows,
    q_mate,
    d_mate,
    out_acc,
    dq_acc,
    dq_mate,
    low_slope,
    low_prob,
    stats_out,
    stats_in,
    inverse,
    row_dots,
    bounds,
    spread,
    part,
    ring_out,
    ring_in,
    y_in,
    rows_out,
    rows_in,
    g_ring_send,
    g_ring_recv,
    g_y_send,
    g_y_recv,
    r_ring_send,
    r_ring_recv,
    r_y_send,
    r_y_recv,
    mate_send,
    mate_recv,
    rows_send,
    rows_recv,
    ready,
):
    lanes = queries.shape[1]
    heads = lanes // HEAD_SIZE
    devices = 2 * RING * ROWS_Y
    index = lax.axis_index("ctx")
    core = lax.rem(index, 2)
    z = lax.rem(lax.div(index, 2), RING)
    h = lax.div(index, 2 * RING)
    sibling = index + 1 - 2 * core
    scale = 1.0 / math.sqrt(HEAD_SIZE)

    def along(place):
        return 2 * RING * h + 2 * lax.rem(place + RING, RING) + core

    barrier = pltpu.get_barrier_semaphore()
    ring_mates = [along(z + step) for step in range(1, RING)]
    column_mates = [
        lax.rem(index - core + 2 * RING * step + lax.rem(core + side, 2), devices)
        for step in range(ROWS_Y)
        for side in (0, 1)
        if step or side
    ]
    for mate in ring_mates + column_mates:
        pl.semaphore_signal(barrier, inc=1, device_id={"ctx": mate}, device_id_type=MESH)

    kv[z, 0] = keys[...]
    kv[z, 1] = values[...]
    pl.semaphore_wait(barrier, len(ring_mates + column_mates))

    def gather_ring(row, origin, shift):
        unit = kv.at[row * RING + origin]
        return send(
            unit,
            unit,
            g_ring_send.at[row, PORT[shift]],
            g_ring_recv.at[row * RING + origin],
            along(origin + shift),
        )

    def to_mate(src, dst, which):
        return send(src, dst, mate_send.at[which], mate_recv.at[which], sibling)

    queries_to_mate = to_mate(queries, q_mate, 0)
    cotangent_to_mate = to_mate(cotangent, d_mate, 1)
    stats_to_mate = to_mate(stats_out, stats_in, 2)
    grads_to_mate = to_mate(dq_acc.at[:, pl.ds(lanes, lanes)], dq_mate, 3)

    def gather_y(step):
        return send(
            kv.at[z],
            kv.at[step * RING + z],
            g_y_send.at[step - 1],
            g_y_recv.at[step - 1],
            lax.rem(index + step * 2 * RING, devices),
        )

    def reduce_ring(row, origin, shift):
        stop = 0 if abs(shift) <= 2 else (2 if shift > 0 else -2)
        return send(
            ring_out.at[row * RING + origin],
            ring_in.at[row, PORT[shift]],
            r_ring_send.at[row * RING + origin],
            r_ring_recv.at[row, PORT[shift]],
            along(origin + stop),
        )

    def reduce_y(step):
        return send(
            ring_out.at[step * RING + z],
            y_in.at[step - 1],
            r_y_send.at[step - 1],
            r_y_recv.at[step - 1],
            lax.rem(index + (ROWS_Y - step) * 2 * RING, devices),
        )

    @pl.when(h + 1 < ROWS_Y)
    def _():
        gather_y(1).start()

    def origin_of(shift):
        return lax.rem(z - shift + RING, RING)

    def further_of(shift):
        if abs(shift) != 2:
            return ()
        return (3, 4) if shift > 0 else (-3, -4)

    def arrive(row, distance):
        if distance == 0:
            if row:
                gather_y(row).wait_recv()
            for shift in (2, -2, 1, -1):

                @pl.when(reaches(row, z, shift, core))
                def _():
                    gather_ring(row, z, shift).start()

            return
        for shift in (distance, -distance):
            origin = origin_of(shift)

            @pl.when(reaches(row, origin, shift, core))
            def _():
                gather_ring(row, origin, shift).wait_recv()
                for further in further_of(shift):

                    @pl.when(reaches(row, origin, further, core))
                    def _():
                        gather_ring(row, origin, further).start()

    arrive(*GATHER_ORDER[0])
    queries_to_mate.start()
    cotangent_to_mate.start()

    @pl.when(h + 1 < ROWS_Y)
    def _():
        gather_y(1).wait_send()

    @pl.when(h + 2 < ROWS_Y)
    def _():
        gather_y(2).start()

    for mate in column_mates:
        pl.semaphore_signal(ready, inc=1, device_id={"ctx": mate}, device_id_type=MESH)

    def lay_out(first, rows_q, rows_d):
        for n in range(heads):
            cols = slice(n * HEAD_SIZE, (n + 1) * HEAD_SIZE)
            to = slice(first + n * HEAD_SIZE, first + (n + 1) * HEAD_SIZE)
            q_t[:, to] = rows_q[:, cols].astype(F32).T.astype(BF16)
            d_t[:, to] = rows_d[:, cols].astype(F32).T.astype(BF16)
            q_rows[to, :] = rows_q[:, cols]
            d_rows[to, :] = rows_d[:, cols]

    lay_out(0, queries, cotangent)
    out_acc[...] = jnp.zeros_like(out_acc)
    dq_acc[...] = jnp.zeros_like(dq_acc)
    lane = lax.broadcasted_iota(jnp.int32, (8, TOK), 1)
    position = jnp.concatenate([index * TOK + lane, sibling * TOK + lane], axis=1)
    start = jnp.zeros((8, 2 * TOK), jnp.int32)
    first = jnp.int32(0)
    for doc in range(lengths.shape[0]):
        start = jnp.where(position >= first, jnp.maximum(start, first), start)
        first = first + lengths[doc]
    bounds[0] = start
    bounds[1] = position
    queries_to_mate.wait_recv()
    cotangent_to_mate.wait_recv()
    lay_out(lanes, q_mate, d_mate)

    def member(row, distance, i):
        origin = lax.rem(z + RING + (2 * i - 1) * distance, RING)
        valid = (h >= row) & needed(row, origin, z) & ((i == 0) | ((distance != 0) & (distance != 4)))
        kept = jnp.where(row == 1, RING + origin, jnp.where((row == 2) & (origin == z), 2 * RING, origin))
        return origin, row * RING + origin, kept, valid

    def statistics(row, origin, slot, kept):
        value_t = jnp.concatenate(
            [kv[slot, 1].astype(F32).T.astype(BF16), jnp.ones((SUM_ROWS, TOK), BF16)], axis=0
        )
        key_first = (((h - row) * RING + origin) * 2 + core) * TOK
        key_at = key_first + lax.broadcasted_iota(jnp.int32, (TOK, 2 * TOK), 0)
        visible = (key_at >= bounds[0, :1]) & (key_at <= bounds[1, :1])
        seen = jnp.concatenate([visible[:, :TOK]] * heads + [visible[:, TOK:]] * heads, axis=1)
        bent = jnp.tanh(dot(kv[slot, 0], q_t[...]) * (scale / SOFTCAP))
        weight = jnp.where(seen, jnp.exp2(bent * (SOFTCAP * math.log2(math.e))), 0.0)
        exps[kept] = weight
        slopes[kept] = weight - weight * bent * bent
        out_acc[...] += dot(value_t, weight.astype(BF16))

    def gather_step(g, carry):
        for i in range(1, len(GATHER_ORDER)):

            @pl.when((g == i) & (h >= GATHER_ORDER[i][0]))
            def _():
                arrive(*GATHER_ORDER[i])

        row = pick(g - 1, [r for r, _ in GATHER_ORDER])
        distance = pick(g - 1, [d for _, d in GATHER_ORDER])

        def one(i, carry):
            origin, slot, kept, valid = member(row, distance, i)

            @pl.when(valid)
            def _():
                statistics(row, origin, slot, kept)

            return carry

        return lax.fori_loop(0, 2, one, carry)

    lax.fori_loop(1, len(GATHER_ORDER) + 1, gather_step, 0)

    dots = jnp.sum(out_acc[:HEAD_SIZE, :] * d_t[...].astype(F32), axis=0, keepdims=True)
    stats_out[0] = out_acc[HEAD_SIZE : HEAD_SIZE + 8, :]
    stats_out[1] = jnp.broadcast_to(dots, (8, 2 * lanes))
    stats_to_mate.start()

    picked = (lax.broadcasted_iota(jnp.int32, (TOK, TOK), 0) == order[...]).astype(F32).T.astype(BF16)
    target = lax.broadcasted_iota(jnp.int32, (TOK * PAD, TOK), 0)
    source = PAD * lax.broadcasted_iota(jnp.int32, (TOK * PAD, TOK), 1)
    for n in range(heads):
        place = (target == source + n).astype(F32).astype(BF16)
        spread[:, n * HEAD_SIZE : (n + 1) * HEAD_SIZE] = dot(place, picked).astype(BF16)

    stats_to_mate.wait_recv()
    mine, other = slice(0, lanes), slice(lanes, 2 * lanes)
    for here, there in ((mine, other), (other, mine)):
        inverse_sum = 1.0 / (stats_out[0, :, here] + stats_in[0, :, there])
        inverse[:, here] = inverse_sum
        row_dots[:, here] = (stats_out[1, :, here] + stats_in[1, :, there]) * inverse_sum

    def gradients(slot, kept):
        key_t = kv[slot, 0].astype(F32).T.astype(BF16)
        inv = inverse[:1, :]
        dots = (dot(kv[slot, 1], d_t[...]) - row_dots[:1, :]) * inv
        slope = (slopes[kept] * dots).astype(BF16)
        low_slope[...] = slope
        low_prob[...] = (exps[kept] * inv).astype(BF16)
        dq_acc[...] += dot(key_t, slope)
        part[slot, 0] = dot(low_slope[...], q_rows[...])
        part[slot, 1] = dot(low_prob[...], d_rows[...])

    def combine(row, distance):
        if distance == 0:
            slot = row * RING + z
            for shift in (1, -1, 2, -2):

                @pl.when(reaches(row, z, shift, core))
                def _():
                    reduce_ring(row, z, shift).wait_recv()
                    part[slot] = part[slot] + ring_in[row, PORT[shift]].astype(F32)

            if row:
                ring_out[slot] = part[slot].astype(BF16)
                reduce_y(row).start()
            return
        for shift in (distance, -distance):
            origin = origin_of(shift)
            slot = row * RING + origin

            @pl.when(reaches(row, origin, shift, core))
            def _():
                if distance == 2:

                    @pl.when(jnp.logical_not(needed(row, origin, z)))
                    def _():
                        part[slot] = jnp.zeros(part.shape[1:], F32)

                for further in further_of(shift):

                    @pl.when(reaches(row, origin, further, core))
                    def _():
                        reduce_ring(row, origin, further).wait_recv()
                        part[slot] = part[slot] + ring_in[row, PORT[further]].astype(F32)

                ring_out[slot] = part[slot].astype(BF16)
                reduce_ring(row, origin, shift).start()

    def reduce_step(g, carry):
        row = pick(g, [r for r, _ in REDUCE_ORDER])
        distance = pick(g, [d for _, d in REDUCE_ORDER])

        def one(i, carry):
            _, slot, kept, valid = member(row, distance, i)

            @pl.when(valid)
            def _():
                gradients(slot, kept)

            return carry

        carry = lax.fori_loop(0, 2, one, carry)
        for i, (row_at, distance_at) in enumerate(REDUCE_ORDER):
            if distance_at:

                @pl.when((g == i) & (h >= row_at))
                def _():
                    combine(row_at, distance_at)

        return carry

    lax.fori_loop(0, len(REDUCE_ORDER), reduce_step, 0)

    grads_to_mate.start()
    grads_to_mate.wait_recv()
    grad_t = ((dq_acc[:, mine] + dq_mate[...]) * scale).astype(BF16)
    moved = dot(spread[...], grad_t, ((1,), (1,))).astype(BF16)
    rows_out[...] = moved.reshape(rows_out.shape)

    pl.semaphore_wait(ready, len(column_mates))

    def rows_to(step, carry):
        owner = lax.rem(index + step, devices)
        send(rows_out.at[owner], rows_in.at[index], rows_send, rows_recv, owner).start()
        return carry

    lax.fori_loop(1, devices, rows_to, 0)
    rows_in[index] = rows_out[index]

    for row in (2, 1, 0):

        @pl.when(h >= row)
        def _():
            combine(row, 0)

    for step in (1, 2):

        @pl.when(h + step < ROWS_Y)
        def _():
            reduce_y(step).wait_recv()
            part[z] = part[z] + y_in[step - 1].astype(F32)

    dk_out[...] = (part[z, 0] * scale).astype(BF16)
    dv_out[...] = part[z, 1].astype(BF16)

    @pl.when(h + 2 < ROWS_Y)
    def _():
        gather_y(2).wait_send()

    for step in (1, 2):

        @pl.when(h >= step)
        def _():
            reduce_y(step).wait_send()

    for row in range(3):

        @pl.when(h >= row)
        def _():
            for shift in PORT:
                origin = origin_of(shift)
                if abs(shift) <= 2:

                    @pl.when(reaches(row, z, shift, core))
                    def _():
                        gather_ring(row, z, shift).wait_send()

                for further in further_of(shift):

                    @pl.when(reaches(row, origin, further, core))
                    def _():
                        gather_ring(row, origin, further).wait_send()

                @pl.when(reaches(row, origin, shift, core))
                def _():
                    reduce_ring(row, origin, shift).wait_send()

    for copy in (queries_to_mate, cotangent_to_mate, stats_to_mate, grads_to_mate):
        copy.wait_send()
    others = pl.ds(0, devices - 1)
    everyone = send(rows_out.at[others], rows_in.at[others], rows_send, rows_recv, sibling)
    everyone.wait_recv()
    everyone.wait_send()
    dq_out[...] = rows_in[...]


def run_kernel(queries, cotangent, keys, values, lengths, order):
    lanes = queries.shape[1]
    devices = lax.axis_size("ctx")
    vmem = pl.BlockSpec(memory_space=pltpu.VMEM)
    block = (2, TOK, HEAD_SIZE)
    travelling = (devices, TOK // devices * PAD, HEAD_SIZE)
    dma = pltpu.SemaphoreType.DMA
    return pl.pallas_call(
        kernel,
        out_shape=(
            jax.ShapeDtypeStruct(travelling, BF16),
            jax.ShapeDtypeStruct((TOK, HEAD_SIZE), BF16),
            jax.ShapeDtypeStruct((TOK, HEAD_SIZE), BF16),
        ),
        in_specs=[pl.BlockSpec(memory_space=pltpu.SMEM)] + [vmem] * 5,
        out_specs=(vmem, vmem, vmem),
        scratch_shapes=[
            pltpu.VMEM((SLOTS,) + block, BF16),
            pltpu.VMEM((HELD, TOK, 2 * lanes), F32),
            pltpu.VMEM((HELD, TOK, 2 * lanes), F32),
            pltpu.VMEM((HEAD_SIZE, 2 * lanes), BF16),
            pltpu.VMEM((HEAD_SIZE, 2 * lanes), BF16),
            pltpu.VMEM((2 * lanes, HEAD_SIZE), BF16),
            pltpu.VMEM((2 * lanes, HEAD_SIZE), BF16),
            pltpu.VMEM((TOK, lanes), BF16),
            pltpu.VMEM((TOK, lanes), BF16),
            pltpu.VMEM((HEAD_SIZE + SUM_ROWS, 2 * lanes), F32),
            pltpu.VMEM((HEAD_SIZE, 2 * lanes), F32),
            pltpu.VMEM((HEAD_SIZE, lanes), F32),
            pltpu.VMEM((TOK, 2 * lanes), BF16),
            pltpu.VMEM((TOK, 2 * lanes), BF16),
            pltpu.VMEM((2, 8, 2 * lanes), F32),
            pltpu.VMEM((2, 8, 2 * lanes), F32),
            pltpu.VMEM((8, 2 * lanes), F32),
            pltpu.VMEM((8, 2 * lanes), F32),
            pltpu.VMEM((2, 8, 2 * TOK), jnp.int32),
            pltpu.VMEM((TOK * PAD, lanes), BF16),
            pltpu.VMEM((SLOTS,) + block, F32),
            pltpu.VMEM((SLOTS,) + block, BF16),
            pltpu.VMEM((3, len(PORT)) + block, BF16),
            pltpu.VMEM((2,) + block, BF16),
            pltpu.VMEM(travelling, BF16),
            pltpu.VMEM(travelling, BF16),
            dma((3, len(PORT))),
            dma((SLOTS,)),
            dma((2,)),
            dma((2,)),
            dma((SLOTS,)),
            dma((3, len(PORT))),
            dma((2,)),
            dma((2,)),
            dma((4,)),
            dma((4,)),
            dma,
            dma,
            pltpu.SemaphoreType.REGULAR,
        ],
        compiler_params=pltpu.CompilerParams(
            collective_id=0, has_side_effects=True, vmem_limit_bytes=58 * 1024 * 1024
        ),
        name="attention_backward",
    )(lengths, order, queries, cotangent, keys, values)


def on_device(queries, keys, values, output_cotangent, lengths, send_order):
    rows, lanes = queries.shape
    moved, dk, dv = run_kernel(queries, output_cotangent, keys, values, lengths, send_order)
    dq_owned = moved.reshape(rows, PAD, HEAD_SIZE)[:, : lanes // HEAD_SIZE]
    return dq_owned.reshape(rows, lanes), dk, dv


def solution(mesh):
    return jax.shard_map(
        on_device,
        mesh=mesh,
        in_specs=(
            P("ctx", "head"),
            P("ctx", "head"),
            P("ctx", "head"),
            P("ctx", "head"),
            P(),
            P("ctx", None),
        ),
        out_specs=(P("ctx", "head"), P("ctx", "head"), P("ctx", "head")),
        check_vma=False,
    )
```

```python
import functools
import math

import jax
import jax.numpy as jnp
from jax import lax
from jax.experimental import pallas as pl
from jax.experimental.pallas import tpu as pltpu
from jax.sharding import PartitionSpec as P

HEAD_SIZE = 128
SOFTCAP = 30
TOK = 128
ROWS_Y = 4
RING = 8
SLOTS = 3 * RING
SUM_ROWS = 16
HELD = 17
PAD = 8
GATHER_ORDER = (
    (0, 0), (1, 0), (0, 2), (2, 0), (1, 2), (0, 1), (2, 2), (1, 1), (2, 1), (0, 3), (1, 3), (0, 4), (1, 4), (2, 3), (2, 4)
)
REDUCE_ORDER = (
    (2, 4), (2, 3), (1, 4), (1, 3), (2, 1), (0, 4), (0, 3), (1, 1), (0, 1), (2, 2), (1, 2), (0, 2), (2, 0), (1, 0), (0, 0)
)
PORT = {1: 0, 2: 1, -1: 2, -2: 3, 3: 4, 4: 5, -3: 6, -4: 7}
MESH = pl.DeviceIdType.MESH
F32 = jnp.float32
BF16 = jnp.bfloat16


def dot(a, b, contract=((1,), (0,))):
    return lax.dot_general(a, b, (contract, ((), ())), preferred_element_type=F32)


def send(src, dst, send_sem, recv_sem, target):
    return pltpu.make_async_remote_copy(
        src_ref=src,
        dst_ref=dst,
        send_sem=send_sem,
        recv_sem=recv_sem,
        device_id={"ctx": target},
        device_id_type=MESH,
    )


def needed(row, origin, z):
    return (row == 1) | ((row == 0) & (origin <= z)) | ((row == 2) & (origin >= z))


def reaches(row, origin, shift, core):
    z = lax.rem(origin + shift + RING, RING)
    if abs(shift) == 4:
        if row == 1:
            return core == (0 if shift > 0 else 1)
        return needed(row, origin, z) & ((row == 0) == (shift > 0))
    wanted = needed(row, origin, z)
    if abs(shift) == 2:
        for further in (3, 4):
            wanted = wanted | reaches(row, origin, further if shift > 0 else -further, core)
    return wanted


def pick(index, table):
    value = jnp.int32(table[0])
    for i in range(1, len(table)):
        value = jnp.where(index == i, table[i], value)
    return value


def kernel(
    lengths,
    order,
    queries,
    cotangent,
    keys,
    values,
    dq_out,
    dk_out,
    dv_out,
    kv,
    exps,
    slopes,
    q_t,
    d_t,
    q_rows,
    d_rows,
    q_mate,
    d_mate,
    out_acc,
    dq_acc,
    dq_mate,
    low_slope,
    low_prob,
    stats_out,
    stats_in,
    inverse,
    row_dots,
    bounds,
    spread,
    part,
    ring_out,
    ring_in,
    y_in,
    rows_out,
    rows_in,
    g_ring_send,
    g_ring_recv,
    g_y_send,
    g_y_recv,
    r_ring_send,
    r_ring_recv,
    r_y_send,
    r_y_recv,
    mate_send,
    mate_recv,
    rows_send,
    rows_recv,
    ready,
):
    lanes = queries.shape[1]
    heads = lanes // HEAD_SIZE
    devices = 2 * RING * ROWS_Y
    index = lax.axis_index("ctx")
    core = lax.rem(index, 2)
    z = lax.rem(lax.div(index, 2), RING)
    h = lax.div(index, 2 * RING)
    sibling = index + 1 - 2 * core
    scale = 1.0 / math.sqrt(HEAD_SIZE)

    def along(place):
        return 2 * RING * h + 2 * lax.rem(place + RING, RING) + core

    barrier = pltpu.get_barrier_semaphore()
    ring_mates = [along(z + step) for step in range(1, RING)]
    column_mates = [
        lax.rem(index - core + 2 * RING * step + lax.rem(core + side, 2), devices)
        for step in range(ROWS_Y)
        for side in (0, 1)
        if step or side
    ]
    for mate in ring_mates + column_mates:
        pl.semaphore_signal(barrier, inc=1, device_id={"ctx": mate}, device_id_type=MESH)

    kv[z, 0] = keys[...]
    kv[z, 1] = values[...]
    pl.semaphore_wait(barrier, len(ring_mates + column_mates))

    def gather_ring(row, origin, shift):
        unit = kv.at[row * RING + origin]
        return send(
            unit,
            unit,
            g_ring_send.at[row, PORT[shift]],
            g_ring_recv.at[row * RING + origin],
            along(origin + shift),
        )

    def to_mate(src, dst, which):
        return send(src, dst, mate_send.at[which], mate_recv.at[which], sibling)

    queries_to_mate = to_mate(queries, q_mate, 0)
    cotangent_to_mate = to_mate(cotangent, d_mate, 1)
    stats_to_mate = to_mate(stats_out, stats_in, 2)
    grads_to_mate = to_mate(dq_acc.at[:, pl.ds(lanes, lanes)], dq_mate, 3)

    def gather_y(step):
        return send(
            kv.at[z],
            kv.at[step * RING + z],
            g_y_send.at[step - 1],
            g_y_recv.at[step - 1],
            lax.rem(index + step * 2 * RING, devices),
        )

    def reduce_ring(row, origin, shift):
        stop = 0 if abs(shift) <= 2 else (2 if shift > 0 else -2)
        return send(
            ring_out.at[row * RING + origin],
            ring_in.at[row, PORT[shift]],
            r_ring_send.at[row * RING + origin],
            r_ring_recv.at[row, PORT[shift]],
            along(origin + stop),
        )

    def reduce_y(step):
        return send(
            ring_out.at[step * RING + z],
            y_in.at[step - 1],
            r_y_send.at[step - 1],
            r_y_recv.at[step - 1],
            lax.rem(index + (ROWS_Y - step) * 2 * RING, devices),
        )

    @pl.when(h + 1 < ROWS_Y)
    def _():
        gather_y(1).start()

    def origin_of(shift):
        return lax.rem(z - shift + RING, RING)

    def further_of(shift):
        if abs(shift) != 2:
            return ()
        return (3, 4) if shift > 0 else (-3, -4)

    def arrive(row, distance):
        if distance == 0:
            if row:
                gather_y(row).wait_recv()
            for shift in (2, -2, 1, -1):

                @pl.when(reaches(row, z, shift, core))
                def _():
                    gather_ring(row, z, shift).start()

            return
        for shift in (distance, -distance):
            origin = origin_of(shift)

            @pl.when(reaches(row, origin, shift, core))
            def _():
                gather_ring(row, origin, shift).wait_recv()
                for further in further_of(shift):

                    @pl.when(reaches(row, origin, further, core))
                    def _():
                        gather_ring(row, origin, further).start()

    arrive(*GATHER_ORDER[0])
    queries_to_mate.start()
    cotangent_to_mate.start()

    @pl.when(h + 1 < ROWS_Y)
    def _():
        gather_y(1).wait_send()

    @pl.when(h + 2 < ROWS_Y)
    def _():
        gather_y(2).start()

    for mate in column_mates:
        pl.semaphore_signal(ready, inc=1, device_id={"ctx": mate}, device_id_type=MESH)

    def lay_out(first, rows_q, rows_d):
        for n in range(heads):
            cols = slice(n * HEAD_SIZE, (n + 1) * HEAD_SIZE)
            to = slice(first + n * HEAD_SIZE, first + (n + 1) * HEAD_SIZE)
            q_t[:, to] = rows_q[:, cols].astype(F32).T.astype(BF16)
            d_t[:, to] = rows_d[:, cols].astype(F32).T.astype(BF16)
            q_rows[to, :] = rows_q[:, cols]
            d_rows[to, :] = rows_d[:, cols]

    lay_out(0, queries, cotangent)
    out_acc[...] = jnp.zeros_like(out_acc)
    dq_acc[...] = jnp.zeros_like(dq_acc)
    lane = lax.broadcasted_iota(jnp.int32, (8, TOK), 1)
    position = jnp.concatenate([index * TOK + lane, sibling * TOK + lane], axis=1)
    start = jnp.zeros((8, 2 * TOK), jnp.int32)
    first = jnp.int32(0)
    for doc in range(lengths.shape[0]):
        start = jnp.where(position >= first, jnp.maximum(start, first), start)
        first = first + lengths[doc]
    bounds[0] = start
    bounds[1] = position
    queries_to_mate.wait_recv()
    cotangent_to_mate.wait_recv()
    lay_out(lanes, q_mate, d_mate)

    def member(row, distance, i):
        origin = lax.rem(z + RING + (2 * i - 1) * distance, RING)
        valid = (h >= row) & needed(row, origin, z) & ((i == 0) | ((distance != 0) & (distance != 4)))
        kept = jnp.where(row == 1, RING + origin, jnp.where((row == 2) & (origin == z), 2 * RING, origin))
        return origin, row * RING + origin, kept, valid

    def statistics(row, origin, slot, kept):
        value_t = jnp.concatenate(
            [kv[slot, 1].astype(F32).T.astype(BF16), jnp.ones((SUM_ROWS, TOK), BF16)], axis=0
        )
        key_first = (((h - row) * RING + origin) * 2 + core) * TOK
        key_at = key_first + lax.broadcasted_iota(jnp.int32, (TOK, 2 * TOK), 0)
        visible = (key_at >= bounds[0, :1]) & (key_at <= bounds[1, :1])
        seen = jnp.concatenate([visible[:, :TOK]] * heads + [visible[:, TOK:]] * heads, axis=1)
        bent = jnp.tanh(dot(kv[slot, 0], q_t[...]) * (scale / SOFTCAP))
        weight = jnp.where(seen, jnp.exp2(bent * (SOFTCAP * math.log2(math.e))), 0.0)
        exps[kept] = weight
        slopes[kept] = weight - weight * bent * bent
        out_acc[...] += dot(value_t, weight.astype(BF16))

    def gather_step(g, carry):
        for i in range(1, len(GATHER_ORDER)):

            @pl.when((g == i) & (h >= GATHER_ORDER[i][0]))
            def _():
                arrive(*GATHER_ORDER[i])

        row = pick(g - 1, [r for r, _ in GATHER_ORDER])
        distance = pick(g - 1, [d for _, d in GATHER_ORDER])

        def one(i, carry):
            origin, slot, kept, valid = member(row, distance, i)

            @pl.when(valid)
            def _():
                statistics(row, origin, slot, kept)

            return carry

        return lax.fori_loop(0, 2, one, carry)

    lax.fori_loop(1, len(GATHER_ORDER) + 1, gather_step, 0)

    dots = jnp.sum(out_acc[:HEAD_SIZE, :] * d_t[...].astype(F32), axis=0, keepdims=True)
    stats_out[0] = out_acc[HEAD_SIZE : HEAD_SIZE + 8, :]
    stats_out[1] = jnp.broadcast_to(dots, (8, 2 * lanes))
    stats_to_mate.start()

    picked = (lax.broadcasted_iota(jnp.int32, (TOK, TOK), 0) == order[...]).astype(F32).T.astype(BF16)
    target = lax.broadcasted_iota(jnp.int32, (TOK * PAD, TOK), 0)
    source = PAD * lax.broadcasted_iota(jnp.int32, (TOK * PAD, TOK), 1)
    for n in range(heads):
        place = (target == source + n).astype(F32).astype(BF16)
        spread[:, n * HEAD_SIZE : (n + 1) * HEAD_SIZE] = dot(place, picked).astype(BF16)

    stats_to_mate.wait_recv()
    mine, other = slice(0, lanes), slice(lanes, 2 * lanes)
    for here, there in ((mine, other), (other, mine)):
        inverse_sum = 1.0 / (stats_out[0, :, here] + stats_in[0, :, there])
        inverse[:, here] = inverse_sum
        row_dots[:, here] = (stats_out[1, :, here] + stats_in[1, :, there]) * inverse_sum

    def gradients(slot, kept):
        key_t = kv[slot, 0].astype(F32).T.astype(BF16)
        inv = inverse[:1, :]
        dots = (dot(kv[slot, 1], d_t[...]) - row_dots[:1, :]) * inv
        slope = (slopes[kept] * dots).astype(BF16)
        low_slope[...] = slope
        low_prob[...] = (exps[kept] * inv).astype(BF16)
        dq_acc[...] += dot(key_t, slope)
        part[slot, 0] = dot(low_slope[...], q_rows[...])
        part[slot, 1] = dot(low_prob[...], d_rows[...])

    def combine(row, distance):
        if distance == 0:
            slot = row * RING + z
            for shift in (1, -1, 2, -2):

                @pl.when(reaches(row, z, shift, core))
                def _():
                    reduce_ring(row, z, shift).wait_recv()
                    part[slot] = part[slot] + ring_in[row, PORT[shift]].astype(F32)

            if row:
                ring_out[slot] = part[slot].astype(BF16)
                reduce_y(row).start()
            return
        for shift in (distance, -distance):
            origin = origin_of(shift)
            slot = row * RING + origin

            @pl.when(reaches(row, origin, shift, core))
            def _():
                if distance == 2:

                    @pl.when(jnp.logical_not(needed(row, origin, z)))
                    def _():
                        part[slot] = jnp.zeros(part.shape[1:], F32)

                for further in further_of(shift):

                    @pl.when(reaches(row, origin, further, core))
                    def _():
                        reduce_ring(row, origin, further).wait_recv()
                        part[slot] = part[slot] + ring_in[row, PORT[further]].astype(F32)

                ring_out[slot] = part[slot].astype(BF16)
                reduce_ring(row, origin, shift).start()

    def reduce_step(g, carry):
        row = pick(g, [r for r, _ in REDUCE_ORDER])
        distance = pick(g, [d for _, d in REDUCE_ORDER])

        def one(i, carry):
            _, slot, kept, valid = member(row, distance, i)

            @pl.when(valid)
            def _():
                gradients(slot, kept)

            return carry

        carry = lax.fori_loop(0, 2, one, carry)
        for i, (row_at, distance_at) in enumerate(REDUCE_ORDER):
            if distance_at:

                @pl.when((g == i) & (h >= row_at))
                def _():
                    combine(row_at, distance_at)

        return carry

    lax.fori_loop(0, len(REDUCE_ORDER), reduce_step, 0)

    grads_to_mate.start()
    for row in (2,):

        @pl.when(h >= row)
        def _():
            combine(row, 0)

    grads_to_mate.wait_recv()
    grad_t = ((dq_acc[:, mine] + dq_mate[...]) * scale).astype(BF16)
    moved = dot(spread[...], grad_t, ((1,), (1,))).astype(BF16)
    rows_out[...] = moved.reshape(rows_out.shape)

    pl.semaphore_wait(ready, len(column_mates))

    def rows_to(step, carry):
        owner = lax.rem(index + step, devices)
        send(rows_out.at[owner], rows_in.at[index], rows_send, rows_recv, owner).start()
        return carry

    lax.fori_loop(1, devices, rows_to, 0)
    rows_in[index] = rows_out[index]

    for row in (1, 0):

        @pl.when(h >= row)
        def _():
            combine(row, 0)

    for step in (1, 2):

        @pl.when(h + step < ROWS_Y)
        def _():
            reduce_y(step).wait_recv()
            part[z] = part[z] + y_in[step - 1].astype(F32)

    dk_out[...] = (part[z, 0] * scale).astype(BF16)
    dv_out[...] = part[z, 1].astype(BF16)

    @pl.when(h + 2 < ROWS_Y)
    def _():
        gather_y(2).wait_send()

    for step in (1, 2):

        @pl.when(h >= step)
        def _():
            reduce_y(step).wait_send()

    for row in range(3):

        @pl.when(h >= row)
        def _():
            for shift in PORT:
                origin = origin_of(shift)
                if abs(shift) <= 2:

                    @pl.when(reaches(row, z, shift, core))
                    def _():
                        gather_ring(row, z, shift).wait_send()

                for further in further_of(shift):

                    @pl.when(reaches(row, origin, further, core))
                    def _():
                        gather_ring(row, origin, further).wait_send()

                @pl.when(reaches(row, origin, shift, core))
                def _():
                    reduce_ring(row, origin, shift).wait_send()

    for copy in (queries_to_mate, cotangent_to_mate, stats_to_mate, grads_to_mate):
        copy.wait_send()
    others = pl.ds(0, devices - 1)
    everyone = send(rows_out.at[others], rows_in.at[others], rows_send, rows_recv, sibling)
    everyone.wait_recv()
    everyone.wait_send()
    dq_out[...] = rows_in[...]


def run_kernel(queries, cotangent, keys, values, lengths, order):
    lanes = queries.shape[1]
    devices = lax.axis_size("ctx")
    vmem = pl.BlockSpec(memory_space=pltpu.VMEM)
    block = (2, TOK, HEAD_SIZE)
    travelling = (devices, TOK // devices * PAD, HEAD_SIZE)
    dma = pltpu.SemaphoreType.DMA
    return pl.pallas_call(
        kernel,
        out_shape=(
            jax.ShapeDtypeStruct(travelling, BF16),
            jax.ShapeDtypeStruct((TOK, HEAD_SIZE), BF16),
            jax.ShapeDtypeStruct((TOK, HEAD_SIZE), BF16),
        ),
        in_specs=[pl.BlockSpec(memory_space=pltpu.SMEM)] + [vmem] * 5,
        out_specs=(vmem, vmem, vmem),
        scratch_shapes=[
            pltpu.VMEM((SLOTS,) + block, BF16),
            pltpu.VMEM((HELD, TOK, 2 * lanes), F32),
            pltpu.VMEM((HELD, TOK, 2 * lanes), F32),
            pltpu.VMEM((HEAD_SIZE, 2 * lanes), BF16),
            pltpu.VMEM((HEAD_SIZE, 2 * lanes), BF16),
            pltpu.VMEM((2 * lanes, HEAD_SIZE), BF16),
            pltpu.VMEM((2 * lanes, HEAD_SIZE), BF16),
            pltpu.VMEM((TOK, lanes), BF16),
            pltpu.VMEM((TOK, lanes), BF16),
            pltpu.VMEM((HEAD_SIZE + SUM_ROWS, 2 * lanes), F32),
            pltpu.VMEM((HEAD_SIZE, 2 * lanes), F32),
            pltpu.VMEM((HEAD_SIZE, lanes), F32),
            pltpu.VMEM((TOK, 2 * lanes), BF16),
            pltpu.VMEM((TOK, 2 * lanes), BF16),
            pltpu.VMEM((2, 8, 2 * lanes), F32),
            pltpu.VMEM((2, 8, 2 * lanes), F32),
            pltpu.VMEM((8, 2 * lanes), F32),
            pltpu.VMEM((8, 2 * lanes), F32),
            pltpu.VMEM((2, 8, 2 * TOK), jnp.int32),
            pltpu.VMEM((TOK * PAD, lanes), BF16),
            pltpu.VMEM((SLOTS,) + block, F32),
            pltpu.VMEM((SLOTS,) + block, BF16),
            pltpu.VMEM((3, len(PORT)) + block, BF16),
            pltpu.VMEM((2,) + block, BF16),
            pltpu.VMEM(travelling, BF16),
            pltpu.VMEM(travelling, BF16),
            dma((3, len(PORT))),
            dma((SLOTS,)),
            dma((2,)),
            dma((2,)),
            dma((SLOTS,)),
            dma((3, len(PORT))),
            dma((2,)),
            dma((2,)),
            dma((4,)),
            dma((4,)),
            dma,
            dma,
            pltpu.SemaphoreType.REGULAR,
        ],
        compiler_params=pltpu.CompilerParams(
            collective_id=0, has_side_effects=True, vmem_limit_bytes=58 * 1024 * 1024
        ),
        name="attention_backward",
    )(lengths, order, queries, cotangent, keys, values)


def on_device(queries, keys, values, output_cotangent, lengths, send_order):
    rows, lanes = queries.shape
    moved, dk, dv = run_kernel(queries, output_cotangent, keys, values, lengths, send_order)
    dq_owned = moved.reshape(rows, PAD, HEAD_SIZE)[:, : lanes // HEAD_SIZE]
    return dq_owned.reshape(rows, lanes), dk, dv


def solution(mesh):
    return jax.shard_map(
        on_device,
        mesh=mesh,
        in_specs=(
            P("ctx", "head"),
            P("ctx", "head"),
            P("ctx", "head"),
            P("ctx", "head"),
            P(),
            P("ctx", None),
        ),
        out_specs=(P("ctx", "head"), P("ctx", "head"), P("ctx", "head")),
        check_vma=False,
    )
```

```python
import functools
import math

import jax
import jax.numpy as jnp
from jax import lax
from jax.experimental import pallas as pl
from jax.experimental.pallas import tpu as pltpu
from jax.sharding import PartitionSpec as P

HEAD_SIZE = 128
SOFTCAP = 30
TOK = 128
ROWS_Y = 4
RING = 8
SLOTS = 3 * RING
SUM_ROWS = 16
HELD = 17
PAD = 8
GATHER_ORDER = (
    (0, 0), (1, 0), (0, 2), (2, 0), (1, 2), (0, 1), (2, 2), (1, 1), (2, 1), (0, 3), (1, 3), (0, 4), (1, 4), (2, 3), (2, 4)
)
REDUCE_ORDER = (
    (2, 4), (2, 3), (1, 4), (1, 3), (2, 1), (0, 4), (0, 3), (1, 1), (0, 1), (2, 2), (1, 2), (0, 2), (2, 0), (1, 0), (0, 0)
)
PORT = {1: 0, 2: 1, -1: 2, -2: 3, 3: 4, 4: 5, -3: 6, -4: 7}
MESH = pl.DeviceIdType.MESH
F32 = jnp.float32
BF16 = jnp.bfloat16


def dot(a, b, contract=((1,), (0,))):
    return lax.dot_general(a, b, (contract, ((), ())), preferred_element_type=F32)


def send(src, dst, send_sem, recv_sem, target):
    return pltpu.make_async_remote_copy(
        src_ref=src,
        dst_ref=dst,
        send_sem=send_sem,
        recv_sem=recv_sem,
        device_id={"ctx": target},
        device_id_type=MESH,
    )


def needed(row, origin, z):
    return (row == 1) | ((row == 0) & (origin <= z)) | ((row == 2) & (origin >= z))


def reaches(row, origin, shift, core):
    z = lax.rem(origin + shift + RING, RING)
    if abs(shift) == 4:
        if row == 1:
            return core == (0 if shift > 0 else 1)
        return needed(row, origin, z) & ((row == 0) == (shift > 0))
    wanted = needed(row, origin, z)
    if abs(shift) == 2:
        for further in (3, 4):
            wanted = wanted | reaches(row, origin, further if shift > 0 else -further, core)
    return wanted


def pick(index, table):
    value = jnp.int32(table[0])
    for i in range(1, len(table)):
        value = jnp.where(index == i, table[i], value)
    return value


def kernel(
    lengths,
    order,
    queries,
    cotangent,
    keys,
    values,
    dq_out,
    dk_out,
    dv_out,
    kv,
    exps,
    slopes,
    q_t,
    d_t,
    q_rows,
    d_rows,
    q_mate,
    d_mate,
    out_acc,
    dq_acc,
    dq_mate,
    low_slope,
    low_prob,
    stats_out,
    stats_in,
    inverse,
    row_dots,
    bounds,
    spread,
    part,
    ring_out,
    ring_in,
    y_in,
    rows_out,
    rows_in,
    g_ring_send,
    g_ring_recv,
    g_y_send,
    g_y_recv,
    r_ring_send,
    r_ring_recv,
    r_y_send,
    r_y_recv,
    mate_send,
    mate_recv,
    rows_send,
    rows_recv,
    ready,
):
    lanes = queries.shape[1]
    heads = lanes // HEAD_SIZE
    devices = 2 * RING * ROWS_Y
    index = lax.axis_index("ctx")
    core = lax.rem(index, 2)
    z = lax.rem(lax.div(index, 2), RING)
    h = lax.div(index, 2 * RING)
    sibling = index + 1 - 2 * core
    scale = 1.0 / math.sqrt(HEAD_SIZE)

    def along(place):
        return 2 * RING * h + 2 * lax.rem(place + RING, RING) + core

    barrier = pltpu.get_barrier_semaphore()
    ring_mates = [along(z + step) for step in range(1, RING)]
    column_mates = [
        lax.rem(index - core + 2 * RING * step + lax.rem(core + side, 2), devices)
        for step in range(ROWS_Y)
        for side in (0, 1)
        if step or side
    ]
    for mate in ring_mates + column_mates:
        pl.semaphore_signal(barrier, inc=1, device_id={"ctx": mate}, device_id_type=MESH)

    kv[z, 0] = keys[...]
    kv[z, 1] = values[...]
    pl.semaphore_wait(barrier, len(ring_mates + column_mates))

    def gather_ring(row, origin, shift):
        unit = kv.at[row * RING + origin]
        return send(
            unit,
            unit,
            g_ring_send.at[row, PORT[shift]],
            g_ring_recv.at[row * RING + origin],
            along(origin + shift),
        )

    def to_mate(src, dst, which):
        return send(src, dst, mate_send.at[which], mate_recv.at[which], sibling)

    queries_to_mate = to_mate(queries, q_mate, 0)
    cotangent_to_mate = to_mate(cotangent, d_mate, 1)
    stats_to_mate = to_mate(stats_out, stats_in, 2)
    grads_to_mate = to_mate(dq_acc.at[:, pl.ds(lanes, lanes)], dq_mate, 3)

    def gather_y(step):
        return send(
            kv.at[z],
            kv.at[step * RING + z],
            g_y_send.at[step - 1],
            g_y_recv.at[step - 1],
            lax.rem(index + step * 2 * RING, devices),
        )

    def reduce_ring(row, origin, shift):
        stop = 0 if abs(shift) <= 2 else (2 if shift > 0 else -2)
        return send(
            ring_out.at[row * RING + origin],
            ring_in.at[row, PORT[shift]],
            r_ring_send.at[row * RING + origin],
            r_ring_recv.at[row, PORT[shift]],
            along(origin + stop),
        )

    def reduce_y(step):
        return send(
            ring_out.at[step * RING + z],
            y_in.at[step - 1],
            r_y_send.at[step - 1],
            r_y_recv.at[step - 1],
            lax.rem(index + (ROWS_Y - step) * 2 * RING, devices),
        )

    @pl.when(h + 1 < ROWS_Y)
    def _():
        gather_y(1).start()

    def origin_of(shift):
        return lax.rem(z - shift + RING, RING)

    def further_of(shift):
        if abs(shift) != 2:
            return ()
        return (3, 4) if shift > 0 else (-3, -4)

    def arrive(row, distance):
        if distance == 0:
            if row:
                gather_y(row).wait_recv()
            for shift in (2, -2, 1, -1):

                @pl.when(reaches(row, z, shift, core))
                def _():
                    gather_ring(row, z, shift).start()

            return
        for shift in (distance, -distance):
            origin = origin_of(shift)

            @pl.when(reaches(row, origin, shift, core))
            def _():
                gather_ring(row, origin, shift).wait_recv()
                for further in further_of(shift):

                    @pl.when(reaches(row, origin, further, core))
                    def _():
                        gather_ring(row, origin, further).start()

    arrive(*GATHER_ORDER[0])
    queries_to_mate.start()
    cotangent_to_mate.start()

    @pl.when(h + 1 < ROWS_Y)
    def _():
        gather_y(1).wait_send()

    @pl.when(h + 2 < ROWS_Y)
    def _():
        gather_y(2).start()

    for mate in column_mates:
        pl.semaphore_signal(ready, inc=1, device_id={"ctx": mate}, device_id_type=MESH)

    def lay_out(first, rows_q, rows_d):
        for n in range(heads):
            cols = slice(n * HEAD_SIZE, (n + 1) * HEAD_SIZE)
            to = slice(first + n * HEAD_SIZE, first + (n + 1) * HEAD_SIZE)
            q_t[:, to] = rows_q[:, cols].astype(F32).T.astype(BF16)
            d_t[:, to] = rows_d[:, cols].astype(F32).T.astype(BF16)
            q_rows[to, :] = rows_q[:, cols]
            d_rows[to, :] = rows_d[:, cols]

    lay_out(0, queries, cotangent)
    out_acc[...] = jnp.zeros_like(out_acc)
    dq_acc[...] = jnp.zeros_like(dq_acc)
    lane = lax.broadcasted_iota(jnp.int32, (8, TOK), 1)
    position = jnp.concatenate([index * TOK + lane, sibling * TOK + lane], axis=1)
    start = jnp.zeros((8, 2 * TOK), jnp.int32)
    first = jnp.int32(0)
    for doc in range(lengths.shape[0]):
        start = jnp.where(position >= first, jnp.maximum(start, first), start)
        first = first + lengths[doc]
    bounds[0] = start
    bounds[1] = position
    queries_to_mate.wait_recv()
    cotangent_to_mate.wait_recv()
    lay_out(lanes, q_mate, d_mate)

    def member(row, distance, i):
        origin = lax.rem(z + RING + (2 * i - 1) * distance, RING)
        valid = (h >= row) & needed(row, origin, z) & ((i == 0) | ((distance != 0) & (distance != 4)))
        kept = jnp.where(row == 1, RING + origin, jnp.where((row == 2) & (origin == z), 2 * RING, origin))
        return origin, row * RING + origin, kept, valid

    def statistics(row, origin, slot, kept):
        value_t = jnp.concatenate(
            [kv[slot, 1].astype(F32).T.astype(BF16), jnp.ones((SUM_ROWS, TOK), BF16)], axis=0
        )
        key_first = (((h - row) * RING + origin) * 2 + core) * TOK
        key_at = key_first + lax.broadcasted_iota(jnp.int32, (TOK, 2 * TOK), 0)
        visible = (key_at >= bounds[0, :1]) & (key_at <= bounds[1, :1])
        seen = jnp.concatenate([visible[:, :TOK]] * heads + [visible[:, TOK:]] * heads, axis=1)
        bent = jnp.tanh(dot(kv[slot, 0], q_t[...]) * (scale / SOFTCAP))
        weight = jnp.where(seen, jnp.exp2(bent * (SOFTCAP * math.log2(math.e))), 0.0)
        exps[kept] = weight
        slopes[kept] = weight - weight * bent * bent
        out_acc[...] += dot(value_t, weight.astype(BF16))

    def gather_step(g, carry):
        for i in range(1, len(GATHER_ORDER)):

            @pl.when((g == i) & (h >= GATHER_ORDER[i][0]))
            def _():
                arrive(*GATHER_ORDER[i])

        row = pick(g - 1, [r for r, _ in GATHER_ORDER])
        distance = pick(g - 1, [d for _, d in GATHER_ORDER])

        def one(i, carry):
            origin, slot, kept, valid = member(row, distance, i)

            @pl.when(valid)
            def _():
                statistics(row, origin, slot, kept)

            return carry

        return lax.fori_loop(0, 2, one, carry)

    lax.fori_loop(1, len(GATHER_ORDER) + 1, gather_step, 0)

    dots = jnp.sum(out_acc[:HEAD_SIZE, :] * d_t[...].astype(F32), axis=0, keepdims=True)
    stats_out[0] = out_acc[HEAD_SIZE : HEAD_SIZE + 8, :]
    stats_out[1] = jnp.broadcast_to(dots, (8, 2 * lanes))
    stats_to_mate.start()

    picked = (lax.broadcasted_iota(jnp.int32, (TOK, TOK), 0) == order[...]).astype(F32).T.astype(BF16)
    target = lax.broadcasted_iota(jnp.int32, (TOK * PAD, TOK), 0)
    source = PAD * lax.broadcasted_iota(jnp.int32, (TOK * PAD, TOK), 1)
    for n in range(heads):
        place = (target == source + n).astype(F32).astype(BF16)
        spread[:, n * HEAD_SIZE : (n + 1) * HEAD_SIZE] = dot(place, picked).astype(BF16)

    stats_to_mate.wait_recv()
    mine, other = slice(0, lanes), slice(lanes, 2 * lanes)
    for here, there in ((mine, other), (other, mine)):
        inverse_sum = 1.0 / (stats_out[0, :, here] + stats_in[0, :, there])
        inverse[:, here] = inverse_sum
        row_dots[:, here] = (stats_out[1, :, here] + stats_in[1, :, there]) * inverse_sum

    def gradients(slot, kept):
        key_t = kv[slot, 0].astype(F32).T.astype(BF16)
        inv = inverse[:1, :]
        dots = (dot(kv[slot, 1], d_t[...]) - row_dots[:1, :]) * inv
        slope = (slopes[kept] * dots).astype(BF16)
        low_slope[...] = slope
        low_prob[...] = (exps[kept] * inv).astype(BF16)
        dq_acc[...] += dot(key_t, slope)
        part[slot, 0] = dot(low_slope[...], q_rows[...])
        part[slot, 1] = dot(low_prob[...], d_rows[...])

    def combine(row, distance):
        if distance == 0:
            slot = row * RING + z
            for shift in (1, -1, 2, -2):

                @pl.when(reaches(row, z, shift, core))
                def _():
                    reduce_ring(row, z, shift).wait_recv()
                    part[slot] = part[slot] + ring_in[row, PORT[shift]].astype(F32)

            if row:
                ring_out[slot] = part[slot].astype(BF16)
                reduce_y(row).start()
            return
        for shift in (distance, -distance):
            origin = origin_of(shift)
            slot = row * RING + origin

            @pl.when(reaches(row, origin, shift, core))
            def _():
                if distance == 2:

                    @pl.when(jnp.logical_not(needed(row, origin, z)))
                    def _():
                        part[slot] = jnp.zeros(part.shape[1:], F32)

                for further in further_of(shift):

                    @pl.when(reaches(row, origin, further, core))
                    def _():
                        reduce_ring(row, origin, further).wait_recv()
                        part[slot] = part[slot] + ring_in[row, PORT[further]].astype(F32)

                ring_out[slot] = part[slot].astype(BF16)
                reduce_ring(row, origin, shift).start()

    def reduce_step(g, carry):
        row = pick(g, [r for r, _ in REDUCE_ORDER])
        distance = pick(g, [d for _, d in REDUCE_ORDER])

        def one(i, carry):
            _, slot, kept, valid = member(row, distance, i)

            @pl.when(valid)
            def _():
                gradients(slot, kept)

            return carry

        carry = lax.fori_loop(0, 2, one, carry)
        for i, (row_at, distance_at) in enumerate(REDUCE_ORDER):
            if distance_at:

                @pl.when((g == i) & (h >= row_at))
                def _():
                    combine(row_at, distance_at)

        return carry

    lax.fori_loop(0, len(REDUCE_ORDER), reduce_step, 0)

    grads_to_mate.start()
    for row in (2,):

        @pl.when(h >= row)
        def _():
            combine(row, 0)

    grads_to_mate.wait_recv()
    grad_t = ((dq_acc[:, mine] + dq_mate[...]) * scale).astype(BF16)
    moved = dot(spread[...], grad_t, ((1,), (1,))).astype(BF16)
    rows_out[...] = moved.reshape(rows_out.shape)

    pl.semaphore_wait(ready, len(column_mates))

    def rows_to(step, carry):
        owner = lax.rem(index + step, devices)
        send(rows_out.at[owner], rows_in.at[index], rows_send, rows_recv, owner).start()
        return carry

    lax.fori_loop(1, devices, rows_to, 0)
    rows_in[index] = rows_out[index]

    for row in (1, 0):

        @pl.when(h >= row)
        def _():
            combine(row, 0)

    for step in (1, 2):

        @pl.when(h + step < ROWS_Y)
        def _():
            reduce_y(step).wait_recv()
            part[z] = part[z] + y_in[step - 1].astype(F32)

    dk_out[...] = (part[z, 0] * scale).astype(BF16)
    dv_out[...] = part[z, 1].astype(BF16)

    @pl.when(h + 2 < ROWS_Y)
    def _():
        gather_y(2).wait_send()

    for step in (1, 2):

        @pl.when(h >= step)
        def _():
            reduce_y(step).wait_send()

    for row in range(3):

        @pl.when(h >= row)
        def _():
            for shift in PORT:
                origin = origin_of(shift)
                if abs(shift) <= 2:

                    @pl.when(reaches(row, z, shift, core))
                    def _():
                        gather_ring(row, z, shift).wait_send()

                for further in further_of(shift):

                    @pl.when(reaches(row, origin, further, core))
                    def _():
                        gather_ring(row, origin, further).wait_send()

                @pl.when(reaches(row, origin, shift, core))
                def _():
                    reduce_ring(row, origin, shift).wait_send()

    for copy in (queries_to_mate, cotangent_to_mate, stats_to_mate, grads_to_mate):
        copy.wait_send()
    others = pl.ds(0, devices - 1)
    everyone = send(rows_out.at[others], rows_in.at[others], rows_send, rows_recv, sibling)
    everyone.wait_recv()
    everyone.wait_send()
    dq_out[...] = rows_in[...]


def run_kernel(queries, cotangent, keys, values, lengths, order):
    lanes = queries.shape[1]
    devices = lax.axis_size("ctx")
    vmem = pl.BlockSpec(memory_space=pltpu.VMEM)
    block = (2, TOK, HEAD_SIZE)
    travelling = (devices, TOK // devices * PAD, HEAD_SIZE)
    dma = pltpu.SemaphoreType.DMA
    return pl.pallas_call(
        kernel,
        out_shape=(
            jax.ShapeDtypeStruct(travelling, BF16),
            jax.ShapeDtypeStruct((TOK, HEAD_SIZE), BF16),
            jax.ShapeDtypeStruct((TOK, HEAD_SIZE), BF16),
        ),
        in_specs=[pl.BlockSpec(memory_space=pltpu.SMEM)] + [vmem] * 5,
        out_specs=(vmem, vmem, vmem),
        scratch_shapes=[
            pltpu.VMEM((SLOTS,) + block, BF16),
            pltpu.VMEM((HELD, TOK, 2 * lanes), F32),
            pltpu.VMEM((HELD, TOK, 2 * lanes), F32),
            pltpu.VMEM((HEAD_SIZE, 2 * lanes), BF16),
            pltpu.VMEM((HEAD_SIZE, 2 * lanes), BF16),
            pltpu.VMEM((2 * lanes, HEAD_SIZE), BF16),
            pltpu.VMEM((2 * lanes, HEAD_SIZE), BF16),
            pltpu.VMEM((TOK, lanes), BF16),
            pltpu.VMEM((TOK, lanes), BF16),
            pltpu.VMEM((HEAD_SIZE + SUM_ROWS, 2 * lanes), F32),
            pltpu.VMEM((HEAD_SIZE, 2 * lanes), F32),
            pltpu.VMEM((HEAD_SIZE, lanes), F32),
            pltpu.VMEM((TOK, 2 * lanes), BF16),
            pltpu.VMEM((TOK, 2 * lanes), BF16),
            pltpu.VMEM((2, 8, 2 * lanes), F32),
            pltpu.VMEM((2, 8, 2 * lanes), F32),
            pltpu.VMEM((8, 2 * lanes), F32),
            pltpu.VMEM((8, 2 * lanes), F32),
            pltpu.VMEM((2, 8, 2 * TOK), jnp.int32),
            pltpu.VMEM((TOK * PAD, lanes), BF16),
            pltpu.VMEM((SLOTS,) + block, F32),
            pltpu.VMEM((SLOTS,) + block, BF16),
            pltpu.VMEM((3, len(PORT)) + block, BF16),
            pltpu.VMEM((2,) + block, BF16),
            pltpu.VMEM(travelling, BF16),
            pltpu.VMEM(travelling, BF16),
            dma((3, len(PORT))),
            dma((SLOTS,)),
            dma((2,)),
            dma((2,)),
            dma((SLOTS,)),
            dma((3, len(PORT))),
            dma((2,)),
            dma((2,)),
            dma((4,)),
            dma((4,)),
            dma,
            dma,
            pltpu.SemaphoreType.REGULAR,
        ],
        compiler_params=pltpu.CompilerParams(
            collective_id=0, has_side_effects=True, vmem_limit_bytes=58 * 1024 * 1024
        ),
        name="attention_backward",
    )(lengths, order, queries, cotangent, keys, values)


def on_device(queries, keys, values, output_cotangent, lengths, send_order):
    rows, lanes = queries.shape
    moved, dk, dv = run_kernel(queries, output_cotangent, keys, values, lengths, send_order)
    padded = moved.reshape(rows, PAD * HEAD_SIZE)
    return padded[:, :lanes], dk, dv


def solution(mesh):
    return jax.shard_map(
        on_device,
        mesh=mesh,
        in_specs=(
            P("ctx", "head"),
            P("ctx", "head"),
            P("ctx", "head"),
            P("ctx", "head"),
            P(),
            P("ctx", None),
        ),
        out_specs=(P("ctx", "head"), P("ctx", "head"), P("ctx", "head")),
        check_vma=False,
    )
```
